32 devices in a mesh: ctx: 8 (over z, x), head: 4 (over y, core).
Axes of the slice: x: 2, y: 2, z: 4, core: 2. Of those that a mesh axis runs over, the one named last changes fastest.
Arguments:
- queries: bfloat16 [1536, 768], P(('ctx', 'head')), may hold values from -2.5 to 2.5
- keys: bfloat16 [1536, 768], P(('ctx', 'head')), may hold values from -2.5 to 2.5
- values: bfloat16 [1536, 768], P(('ctx', 'head')), may hold values from -6 to 6
- attended: bfloat16 [1536, 768], P(('ctx', 'head')), may hold values from -6 to 6
- grad_out: bfloat16 [1536, 768], P(('ctx', 'head')), may hold values from -6 to 6
- logsumexp: float32 [1536, 12], P('ctx', 'head'), may hold values from 5 to 8
Outputs:
- grad_queries: bfloat16 [1536, 768], P(('ctx', 'head'))
- grad_keys: bfloat16 [1536, 768], P(('ctx', 'head'))
- grad_values: bfloat16 [1536, 768], P(('ctx', 'head'))
The draws below stay inside these ranges and needn't reach their ends.
All inputs are finite; a program needn't handle non-finite values.
Results may differ from the reference program's by a relative error of at most 0.0051.
Values may be sent and summed in bfloat16 or wider, within the bound.
No kernel may reach another device: no remote copies, remote signals or barrier semaphores. Data moves between devices by JAX's collectives and lax.ppermute only.
A program may use at most 128 MiB of HBM per device.

```python
import math
import jax
import jax.numpy as jnp
from jax import lax

HEADS = 12
HEAD_DIM = 64
WIDTH = 768
SEQ = 1536


def levels(own_key, extent, pieces, smallest, largest):
    level = 1.0
    for axis_at, parts in pieces:
        heights = jax.random.uniform(jax.random.fold_in(jax.random.fold_in(own_key, 6), axis_at), (parts,), jnp.float32, smallest / len(pieces), largest / len(pieces))
        level = level * jnp.repeat(jnp.exp(heights), extent[axis_at] // parts).reshape((-1,) + (1,) * (len(extent) - 1 - axis_at))
    return level


def scatter_about(key, dims, spread, bound, cuts=(), kind=jnp.bfloat16):
    values = jax.random.normal(key, dims, jnp.float32) * spread
    if len(cuts) > 0:
        values = levels(key, dims, cuts, -0.22, 0.18) * values
    return jnp.clip(values, min=-bound, max=bound).astype(kind)


def setup_inputs(seed: int = 0) -> dict:
    splits = jax.random.split(jax.random.key(seed), 7)
    queries = scatter_about(splits[0], (SEQ, WIDTH), 1.0, 2.5, ((0, 32),))
    keys = scatter_about(splits[1], (SEQ, WIDTH), 1.0, 2.5, ((0, 32),))
    values = scatter_about(splits[2], (SEQ, WIDTH), 1.0, 6.0, ((0, 32),))
    attended = scatter_about(splits[3], (SEQ, WIDTH), 1.0, 6.0, ((0, 32),))
    grad_out = scatter_about(splits[4], (SEQ, WIDTH), 1.0, 6.0, ((0, 32),))
    logsumexp = jnp.clip(5.0 + 3.0 * jax.random.uniform(splits[5], (SEQ, HEADS), jnp.float32) ** levels(splits[5], (SEQ, HEADS), ((0, 8), (1, 4)), -0.2, 0.2), 5.0, 8.0)
    return {"queries": queries, "keys": keys, "values": values, "attended": attended, "grad_out": grad_out, "logsumexp": logsumexp}


def reference(queries, keys, values, attended, grad_out, logsumexp):
    scaling = HEAD_DIM ** -0.5
    length = queries.shape[0]

    def by_head(matrix):
        return matrix.astype(jnp.float32).reshape(length, HEADS, HEAD_DIM)

    local_q = by_head(queries)
    local_k = by_head(keys)
    local_v = by_head(values)
    local_o = by_head(attended)
    local_g = by_head(grad_out)
    deltas = jnp.sum(local_g * local_o, axis=2)
    block_size = math.gcd(length, 256)
    block_count = length // block_size

    def visit(totals, inputs):
        grad_key, grad_value = totals
        query_part, grad_part, norm_part, delta_part = inputs
        scores = jnp.einsum("ahd,bhd->hab", query_part, local_k) * scaling
        weights = jnp.exp(scores - jnp.transpose(norm_part)[:, :, None])
        weights_low = lax.optimization_barrier(weights.astype(jnp.bfloat16)).astype(jnp.float32)
        dweights = jnp.einsum("ahd,bhd->hab", grad_part, local_v)
        dscores = weights * (dweights - jnp.transpose(delta_part)[:, :, None])
        dscores = lax.optimization_barrier(dscores.astype(jnp.bfloat16)).astype(jnp.float32)
        grad_query = jnp.einsum("hab,bhd->ahd", dscores, local_k) * scaling
        grad_key = grad_key + jnp.einsum("hab,ahd->bhd", dscores, query_part) * scaling
        grad_value = grad_value + jnp.einsum("hab,ahd->bhd", weights_low, grad_part)
        return (grad_key, grad_value), grad_query

    zeros = jnp.zeros((length, HEADS, HEAD_DIM), jnp.float32)
    stacked = (
        local_q.reshape(block_count, block_size, HEADS, HEAD_DIM),
        local_g.reshape(block_count, block_size, HEADS, HEAD_DIM),
        logsumexp.reshape(block_count, block_size, HEADS),
        deltas.reshape(block_count, block_size, HEADS),
    )
    totals, grad_query = lax.scan(visit, (zeros, zeros), stacked)

    def finish(matrix):
        return matrix.reshape(length, HEADS * HEAD_DIM).astype(jnp.bfloat16)

    return finish(grad_query), finish(totals[0]), finish(totals[1])
```

```python
import functools
import jax
import jax.numpy as jnp
from jax import lax
from jax.experimental import pallas as pl
from jax.experimental.pallas import tpu as pltpu
from jax.sharding import PartitionSpec as P

F32 = jnp.float32
BF16 = jnp.bfloat16
LANES = 128
NT = (((1,), (1,)), ((), ()))
TN = (((0,), (0,)), ((), ()))
NN = (((1,), (0,)), ((), ()))
VMEM = pl.BlockSpec(memory_space=pltpu.VMEM)


def dot(a, b, dims):
    return lax.dot_general(a, b, dims, preferred_element_type=F32)


def round_up(n, m):
    return -(-n // m) * m


class Sizes:
    def __init__(self, rows, width, heads_group, group, ctx):
        self.rows, self.width = rows, width
        self.group, self.ctx = group, ctx
        self.heads_group = heads_group
        self.heads = heads_group * group
        self.dim = width // self.heads
        self.tiles = width // LANES
        self.span = rows * group
        self.span_tiles = -(-self.span // LANES)
        self.part = self.tiles * rows
        self.lse_rows = 3 * heads_group * self.span_tiles
        self.extra = round_up(self.lse_rows + 2 * self.heads, 16)
        self.high = ctx // 2


def split3(x):
    hi = x.astype(BF16).astype(F32)
    rest = x - hi
    mid = rest.astype(BF16).astype(F32)
    return hi, mid, rest - mid


def pack_kernel(s, q_ref, k_ref, v_ref, o_ref, g_ref, lse_ref, qg_ref, kv_ref, wide, small):
    r = s.rows
    for t in range(s.tiles):
        lanes = slice(t * LANES, (t + 1) * LANES)
        rows = slice(t * r, (t + 1) * r)
        more = slice(s.part + t * r, s.part + (t + 1) * r)
        qg_ref[rows, :] = q_ref[:, lanes]
        qg_ref[more, :] = g_ref[:, lanes]
        kv_ref[rows, :] = k_ref[:, lanes]
        kv_ref[more, :] = v_ref[:, lanes]
    prod = g_ref[...].astype(F32) * o_ref[...].astype(F32)
    hi = prod.astype(BF16)
    lo = (prod - hi.astype(F32)).astype(BF16)
    shape = (round_up(s.heads, 16), s.width)
    pick = lax.broadcasted_iota(jnp.int32, shape, 1) // s.dim
    pick = (pick == lax.broadcasted_iota(jnp.int32, shape, 0)).astype(F32).astype(BF16)
    delta = dot(pick, hi, NT) + dot(pick, lo, NT)
    d_hi, d_mid, _ = split3(delta)
    wide[...] = jnp.zeros(wide.shape, F32)
    wide[: s.span, : s.heads_group] = lse_ref[...]
    lse = wide[...].T[:8]
    small[...] = jnp.zeros(small.shape, F32)
    at = 0
    for t in range(s.span_tiles):
        for piece in split3(lse[:, t * LANES : (t + 1) * LANES]):
            small[at : at + s.heads_group, :] = piece[: s.heads_group]
            at += s.heads_group
    small[at : at + s.heads, : s.rows] = d_hi[: s.heads]
    small[at + s.heads : at + 2 * s.heads, : s.rows] = d_mid[: s.heads]
    qg_ref[2 * s.part :, :] = small[...].astype(BF16)


def pack(s, q, k, v, o, g, lse):
    return pl.pallas_call(
        functools.partial(pack_kernel, s),
        out_shape=(
            jax.ShapeDtypeStruct((2 * s.part + s.extra, LANES), BF16),
            jax.ShapeDtypeStruct((2 * s.part, LANES), BF16),
        ),
        in_specs=[VMEM] * 6,
        out_specs=[VMEM] * 2,
        scratch_shapes=[
            pltpu.VMEM((round_up(s.span, LANES), LANES), F32),
            pltpu.VMEM((s.extra, LANES), F32),
        ],
    )(q, k, v, o, g, lse)


def attend_kernel(s, blocks, first, *refs):
    r, n = s.rows, s.group
    refs = list(refs)
    take = lambda count: [refs.pop(0) for _ in range(count)]
    qg, kv = take(n), take(blocks)
    (old,) = take(1) if not first else (None,)
    keep, (send,) = take(n // 2), take(1)
    sums = take(1 if first else blocks)
    qs, gs, dqs, norms, deltas = refs
    me = lax.axis_index("head")
    scale = s.dim**-0.5
    wide = s.span_tiles * LANES
    h = s.heads_group
    total = jnp.zeros((s.heads, wide), F32)
    for off in range(n):
        who = lax.bitwise_xor(me, off)
        at = pl.multiple_of(who * r, 16)
        for t in range(s.tiles):
            q = qg[off][t * r : (t + 1) * r, :]
            qs[t, pl.ds(at, r), :] = (q.astype(F32) * scale).astype(BF16)
            gs[t, pl.ds(at, r), :] = qg[off][s.part + t * r : s.part + (t + 1) * r, :]
        small = qg[off][2 * s.part :, :].astype(F32)
        pieces = []
        for t in range(s.span_tiles):
            b = 3 * h * t
            pieces.append(small[b : b + h] + small[b + h : b + 2 * h] + small[b + 2 * h : b + 3 * h])
        norms[who, :h, :] = jnp.concatenate(pieces, axis=1)
        b = s.lse_rows
        delta = small[b : b + s.heads] + small[b + s.heads : b + 2 * s.heads]
        if wide > LANES:
            delta = jnp.concatenate([delta, jnp.zeros((s.heads, wide - LANES), F32)], axis=1)
        total = total + pltpu.roll(delta, who * r, 1)
    deltas[...] = total
    half = lax.broadcasted_iota(jnp.int32, (blocks * r, LANES), 1) < s.dim
    zero = jnp.zeros((), BF16)
    for t in range(s.tiles):
        rows = slice(t * r, (t + 1) * r)
        more = slice(s.part + t * r, s.part + (t + 1) * r)
        k = jnp.concatenate([ref[rows, :] for ref in kv], axis=0)
        v = jnp.concatenate([ref[more, :] for ref in kv], axis=0)
        q, g = qs[t], gs[t]
        dk, dv, dq = [], [], None
        for e in range(2):
            head = 2 * t + e
            mask = half if e == 0 else jnp.logical_not(half)
            k_one = jnp.where(mask, k, zero)
            v_one = jnp.where(mask, v, zero)
            j = head % h
            norm = norms[head // h, j : j + 1, : s.span]
            weights = jnp.exp(dot(k_one, q, NT) - norm)
            dweights = dot(v_one, g, NT)
            dscores = (weights * (dweights - deltas[head : head + 1, : s.span])).astype(BF16)
            dv.append(dot(weights.astype(BF16), g, NN))
            dk.append(dot(dscores, q, NN))
            term = dot(dscores, k_one, TN)
            dq = term if dq is None else dq + term
        dqs[t] = dq * scale
        for where, pair in ((rows, dk), (more, dv)):
            both = jnp.where(half, pair[0], pair[1])
            for i in range(blocks):
                piece = both[i * r : (i + 1) * r]
                if first:
                    sums[0][2 * s.part * i + where.start : 2 * s.part * i + where.stop, :] = piece
                else:
                    piece = piece + old[2 * s.part * i + where.start : 2 * s.part * i + where.stop, :]
                    sums[i][where, :] = piece.astype(sums[i].dtype)
    for off in range(n):
        at = pl.multiple_of(lax.bitwise_xor(me, off) * r, 16)
        for t in range(s.tiles):
            piece = dqs[t, pl.ds(at, r), :]
            i = off // 2
            if off % 2 == 0:
                keep[i][t * r : (t + 1) * r, :] = piece
            else:
                send[i * s.part + t * r : i * s.part + (t + 1) * r, :] = piece.astype(BF16)


def attend(s, qg, kv, old):
    blocks = len(kv)
    first = old is None
    out = [jax.ShapeDtypeStruct((s.part, LANES), F32)] * (s.group // 2)
    out.append(jax.ShapeDtypeStruct((s.group // 2 * s.part, LANES), BF16))
    if first:
        out.append(jax.ShapeDtypeStruct((blocks * 2 * s.part, LANES), F32))
    else:
        out.append(jax.ShapeDtypeStruct((2 * s.part, LANES), F32))
        out += [jax.ShapeDtypeStruct((2 * s.part, LANES), BF16)] * (blocks - 1)
    operands = list(qg) + list(kv) + ([] if first else [old])
    pairs = s.heads * s.span * blocks * s.rows
    result = pl.pallas_call(
        functools.partial(attend_kernel, s, blocks, first),
        out_shape=out,
        in_specs=[VMEM] * len(operands),
        out_specs=[VMEM] * len(out),
        scratch_shapes=[
            pltpu.VMEM((s.tiles, s.span, LANES), BF16),
            pltpu.VMEM((s.tiles, s.span, LANES), BF16),
            pltpu.VMEM((s.tiles, s.span, LANES), F32),
            pltpu.VMEM((s.group, 8, s.span_tiles * LANES), F32),
            pltpu.VMEM((s.heads, s.span_tiles * LANES), F32),
        ],
        compiler_params=pltpu.CompilerParams(vmem_limit_bytes=48 * 2**20),
        cost_estimate=pl.CostEstimate(
            flops=20 * pairs * s.dim, bytes_accessed=4 * s.part * LANES * 8, transcendentals=pairs
        ),
    )(*operands)
    count = s.group // 2
    return result[:count], result[count], result[count + 1 :]


def core_kernel(s, keep_own, *refs):
    count = s.group // 2
    recv = refs[count]
    for i in range(count):
        total = refs[i][...] + recv[i * s.part : (i + 1) * s.part, :].astype(F32)
        refs[count + 1 + i][...] = total.astype(refs[count + 1 + i].dtype)


def core_add(s, keep, recv, keep_own):
    count = len(keep)
    out = [
        jax.ShapeDtypeStruct((s.part, LANES), F32 if keep_own and i == 0 else BF16)
        for i in range(count)
    ]
    return pl.pallas_call(
        functools.partial(core_kernel, s, keep_own),
        out_shape=out,
        in_specs=[VMEM] * (count + 1),
        out_specs=[VMEM] * count,
    )(*keep, recv)


def final_kernel(s, n_dq, n_kv, *refs):
    dq, kv = refs[:n_dq], refs[n_dq : n_dq + n_kv]
    outs = refs[n_dq + n_kv :]
    r = s.rows
    for out, sources, base in ((outs[0], dq, 0), (outs[1], kv, 0), (outs[2], kv, s.part)):
        for t in range(s.tiles):
            rows = slice(base + t * r, base + (t + 1) * r)
            total = sources[0][rows, :].astype(F32)
            for ref in sources[1:]:
                total = total + ref[rows, :].astype(F32)
            out[:, t * LANES : (t + 1) * LANES] = total.astype(BF16)


def finish(s, dq, kv):
    return pl.pallas_call(
        functools.partial(final_kernel, s, len(dq), len(kv)),
        out_shape=[jax.ShapeDtypeStruct((s.rows, s.width), BF16)] * 3,
        in_specs=[VMEM] * (len(dq) + len(kv)),
        out_specs=[VMEM] * 3,
    )(*dq, *kv)


def local(queries, keys, values, attended, grad_out, logsumexp):
    group, ctx = lax.axis_size("head"), lax.axis_size("ctx")
    s = Sizes(queries.shape[0], queries.shape[1], logsumexp.shape[1], group, ctx)

    def move(x, ctx_off, head_off):
        if ctx_off == 0:
            return lax.ppermute(x, "head", [(i, i ^ head_off) for i in range(group)])
        if head_off == 0:
            return lax.ppermute(x, "ctx", [(i, i ^ ctx_off) for i in range(ctx)])
        pairs = [
            (i * group + j, (i ^ ctx_off) * group + (j ^ head_off))
            for i in range(ctx)
            for j in range(group)
        ]
        return lax.ppermute(x, ("ctx", "head"), pairs)

    qg_own, kv_own = pack(s, queries, keys, values, attended, grad_out, logsumexp)
    far = {0: move(qg_own, s.high, 0)}
    kv = {0: kv_own}
    bit = s.high // 2
    while bit:
        for off in sorted(kv):
            kv[off + bit] = move(kv[off], bit, 0)
        bit //= 2
    near = {0: qg_own}
    bit = group // 2
    while bit:
        for blocks in (near, far):
            for off in sorted(blocks):
                blocks[off + bit] = move(blocks[off], 0, bit)
        bit //= 2
    kv = [kv[off] for off in range(s.high)]
    keep0, send0, sums0 = attend(s, [near[i] for i in range(group)], kv, None)
    keep1, send1, sums1 = attend(s, [far[i] for i in range(group)], kv, sums0[0])
    dq = core_add(s, keep0, move(send0, 0, 1), True)
    total_q = [dq[0]] + [move(dq[i], 0, 2 * i) for i in range(1, group // 2)]
    dq = core_add(s, keep1, move(send1, 0, 1), False)
    total_q += [move(dq[i], s.high, 2 * i) for i in range(group // 2)]
    total_kv = [sums1[0]] + [move(sums1[off], off, 0) for off in range(1, s.high)]
    return tuple(finish(s, total_q, total_kv))


def solution(mesh):
    rows = P(("ctx", "head"), None)
    return jax.shard_map(
        local,
        mesh=mesh,
        in_specs=(rows, rows, rows, rows, rows, P("ctx", "head")),
        out_specs=(rows, rows, rows),
        check_vma=False,
    )
```

```python
import functools
import jax
import jax.numpy as jnp
from jax import lax
from jax.experimental import pallas as pl
from jax.experimental.pallas import tpu as pltpu
from jax.sharding import PartitionSpec as P

F32 = jnp.float32
BF16 = jnp.bfloat16
LANES = 128
NT = (((1,), (1,)), ((), ()))
TN = (((0,), (0,)), ((), ()))
NN = (((1,), (0,)), ((), ()))
VMEM = pl.BlockSpec(memory_space=pltpu.VMEM)


def dot(a, b, dims):
    return lax.dot_general(a, b, dims, preferred_element_type=F32)


def round_up(n, m):
    return -(-n // m) * m


class Sizes:
    def __init__(self, rows, width, heads_group, group, ctx):
        self.rows, self.width = rows, width
        self.group, self.ctx = group, ctx
        self.heads_group = heads_group
        self.heads = heads_group * group
        self.dim = width // self.heads
        self.tiles = width // LANES
        self.span = rows * group
        self.span_tiles = -(-self.span // LANES)
        self.part = self.tiles * rows
        self.lse_rows = 3 * heads_group * self.span_tiles
        self.extra = round_up(self.lse_rows + 2 * self.heads, 16)
        self.high = ctx // 2

    def grant(self, blocks):
        scratch = 8 * self.tiles * self.span * LANES
        pairs = blocks * self.rows * round_up(self.span, LANES)
        return 2 * scratch + 32 * pairs + 2**20


def split3(x):
    hi = x.astype(BF16).astype(F32)
    rest = x - hi
    mid = rest.astype(BF16).astype(F32)
    return hi, mid, rest - mid


def pack_kernel(s, q_in, k_in, v_in, o_in, g_in, lse_in, qg_ref, kv_ref, *scratch):
    q_ref, k_ref, v_ref, o_ref, g_ref, lse_ref, small, sems = scratch
    copies = [
        pltpu.make_async_copy(source, target, sems.at[i])
        for i, (source, target) in enumerate(
            (
                (g_in, g_ref),
                (o_in, o_ref),
                (lse_in, lse_ref),
                (q_in, q_ref),
                (k_in, k_ref),
                (v_in, v_ref),
            )
        )
    ]
    for copy in copies:
        copy.start()
    r = s.rows
    copies[0].wait()
    copies[1].wait()
    prod = g_ref[...].astype(F32) * o_ref[...].astype(F32)
    hi = prod.astype(BF16)
    lo = (prod - hi.astype(F32)).astype(BF16)
    shape = (round_up(s.heads, 16), s.width)
    pick = lax.broadcasted_iota(jnp.int32, shape, 1) // s.dim
    pick = (pick == lax.broadcasted_iota(jnp.int32, shape, 0)).astype(F32).astype(BF16)
    delta = dot(pick, hi, NT) + dot(pick, lo, NT)
    d_hi, d_mid, _ = split3(delta)
    small[...] = jnp.zeros(small.shape, F32)
    copies[2].wait()
    h = s.heads_group
    at = 0
    for t in range(s.span_tiles):
        lanes = min(LANES, s.span - t * LANES)
        for piece in split3(lse_ref[:, t * LANES : t * LANES + lanes]):
            small[at : at + h, :lanes] = piece
            at += h
    small[at : at + s.heads, :r] = d_hi[: s.heads]
    small[at + s.heads : at + 2 * s.heads, :r] = d_mid[: s.heads]
    qg_ref[2 * s.part :, :] = small[...].astype(BF16)
    for copy in copies[3:]:
        copy.wait()
    for t in range(s.tiles):
        lanes = slice(t * LANES, (t + 1) * LANES)
        rows = slice(t * r, (t + 1) * r)
        more = slice(s.part + t * r, s.part + (t + 1) * r)
        qg_ref[rows, :] = q_ref[:, lanes]
        qg_ref[more, :] = g_ref[:, lanes]
        kv_ref[rows, :] = k_ref[:, lanes]
        kv_ref[more, :] = v_ref[:, lanes]


def in_hbm(x):
    return pltpu.with_memory_space_constraint(x, pltpu.HBM)


def pack(s, q, k, v, o, g, lse):
    return pl.pallas_call(
        functools.partial(pack_kernel, s),
        out_shape=(
            jax.ShapeDtypeStruct((2 * s.part + s.extra, LANES), BF16),
            jax.ShapeDtypeStruct((2 * s.part, LANES), BF16),
        ),
        in_specs=[pl.BlockSpec(memory_space=pl.ANY)] * 6,
        out_specs=[VMEM] * 2,
        scratch_shapes=[pltpu.VMEM((s.rows, s.width), BF16)] * 5
        + [
            pltpu.VMEM((s.heads_group, s.span), F32),
            pltpu.VMEM((s.extra, LANES), F32),
            pltpu.SemaphoreType.DMA((6,)),
        ],
        compiler_params=pltpu.CompilerParams(vmem_limit_bytes=2 * 2**20),
    )(*[in_hbm(x) for x in (q, k, v, o, g, jnp.transpose(lse))])


def attend_kernel(s, blocks, first, *refs):
    r, n = s.rows, s.group
    refs = list(refs)
    take = lambda count: [refs.pop(0) for _ in range(count)]
    qg, kv = take(n), take(blocks)
    (old,) = take(1) if not first else (None,)
    keep, (send,) = take(n // 2), take(1)
    sums = take(1 if first else blocks)
    qs, gs, dqs, norms, deltas = refs
    me = lax.axis_index("head")
    scale = s.dim**-0.5
    wide = s.span_tiles * LANES
    h = s.heads_group
    total = jnp.zeros((s.heads, wide), F32)
    for off in range(n):
        who = lax.bitwise_xor(me, off)
        at = pl.multiple_of(who * r, 16)
        for t in range(s.tiles):
            q = qg[off][t * r : (t + 1) * r, :]
            qs[t, pl.ds(at, r), :] = (q.astype(F32) * scale).astype(BF16)
            gs[t, pl.ds(at, r), :] = qg[off][s.part + t * r : s.part + (t + 1) * r, :]
        small = qg[off][2 * s.part :, :].astype(F32)
        pieces = []
        for t in range(s.span_tiles):
            b = 3 * h * t
            pieces.append(small[b : b + h] + small[b + h : b + 2 * h] + small[b + 2 * h : b + 3 * h])
        norms[who, :h, :] = jnp.concatenate(pieces, axis=1)
        b = s.lse_rows
        delta = small[b : b + s.heads] + small[b + s.heads : b + 2 * s.heads]
        if wide > LANES:
            delta = jnp.concatenate([delta, jnp.zeros((s.heads, wide - LANES), F32)], axis=1)
        total = total + pltpu.roll(delta, who * r, 1)
    deltas[...] = total
    size = blocks * r
    lane = lax.broadcasted_iota(jnp.int32, (2 * size, LANES), 1) < s.dim
    first_head = lax.broadcasted_iota(jnp.int32, (2 * size, LANES), 0) < size
    own_lanes = lane == first_head
    half = lane[:size]
    zero = jnp.zeros((), BF16)

    def pair(block):
        return jnp.where(own_lanes, jnp.concatenate([block, block], axis=0), zero)

    for t in range(s.tiles):
        rows = slice(t * r, (t + 1) * r)
        more = slice(s.part + t * r, s.part + (t + 1) * r)
        k = pair(jnp.concatenate([ref[rows, :] for ref in kv], axis=0))
        v = pair(jnp.concatenate([ref[more, :] for ref in kv], axis=0))
        q, g = qs[t], gs[t]
        scores = dot(k, q, NT)
        dweights = dot(v, g, NT)
        low, dscores = [], []
        for e in range(2):
            head = 2 * t + e
            mine = slice(e * size, (e + 1) * size)
            j = head % h
            weights = jnp.exp(scores[mine] - norms[head // h, j : j + 1, : s.span])
            low.append(weights.astype(BF16))
            gap = dweights[mine] - deltas[head : head + 1, : s.span]
            dscores.append((weights * gap).astype(BF16))
        low = jnp.concatenate(low, axis=0)
        dscores = jnp.concatenate(dscores, axis=0)
        dv = dot(low, g, NN)
        dk = dot(dscores, q, NN)
        dv, dk = [dv[:size], dv[size:]], [dk[:size], dk[size:]]
        dq = dot(dscores, k, TN)
        dqs[t] = dq * scale
        for where, parts in ((rows, dk), (more, dv)):
            both = jnp.where(half, parts[0], parts[1])
            for i in range(blocks):
                piece = both[i * r : (i + 1) * r]
                if first:
                    sums[0][2 * s.part * i + where.start : 2 * s.part * i + where.stop, :] = piece
                else:
                    piece = piece + old[2 * s.part * i + where.start : 2 * s.part * i + where.stop, :]
                    sums[i][where, :] = piece.astype(sums[i].dtype)
    for off in range(n):
        at = pl.multiple_of(lax.bitwise_xor(me, off) * r, 16)
        for t in range(s.tiles):
            piece = dqs[t, pl.ds(at, r), :]
            i = off // 2
            if off % 2 == 0:
                keep[i][t * r : (t + 1) * r, :] = piece
            else:
                send[i * s.part + t * r : i * s.part + (t + 1) * r, :] = piece.astype(BF16)


def attend(s, qg, kv, old):
    blocks = len(kv)
    first = old is None
    out = [jax.ShapeDtypeStruct((s.part, LANES), F32)] * (s.group // 2)
    out.append(jax.ShapeDtypeStruct((s.group // 2 * s.part, LANES), BF16))
    if first:
        out.append(jax.ShapeDtypeStruct((blocks * 2 * s.part, LANES), F32))
    else:
        out.append(jax.ShapeDtypeStruct((2 * s.part, LANES), F32))
        out += [jax.ShapeDtypeStruct((2 * s.part, LANES), BF16)] * (blocks - 1)
    operands = list(qg) + list(kv) + ([] if first else [old])
    pairs = s.heads * s.span * blocks * s.rows
    result = pl.pallas_call(
        functools.partial(attend_kernel, s, blocks, first),
        out_shape=out,
        in_specs=[VMEM] * len(operands),
        out_specs=[VMEM] * len(out),
        scratch_shapes=[
            pltpu.VMEM((s.tiles, s.span, LANES), BF16),
            pltpu.VMEM((s.tiles, s.span, LANES), BF16),
            pltpu.VMEM((s.tiles, s.span, LANES), F32),
            pltpu.VMEM((s.group, 8, s.span_tiles * LANES), F32),
            pltpu.VMEM((s.heads, s.span_tiles * LANES), F32),
        ],
        compiler_params=pltpu.CompilerParams(vmem_limit_bytes=s.grant(blocks)),
        cost_estimate=pl.CostEstimate(
            flops=200 * pairs * s.dim, bytes_accessed=4 * s.part * LANES * 8, transcendentals=pairs
        ),
    )(*operands)
    count = s.group // 2
    return result[:count], result[count], result[count + 1 :]


def core_kernel(s, keep_own, *refs):
    count = s.group // 2
    recv = refs[count]
    for i in range(count):
        total = refs[i][...] + recv[i * s.part : (i + 1) * s.part, :].astype(F32)
        refs[count + 1 + i][...] = total.astype(refs[count + 1 + i].dtype)


def core_add(s, keep, recv, keep_own):
    count = len(keep)
    out = [
        jax.ShapeDtypeStruct((s.part, LANES), F32 if keep_own and i == 0 else BF16)
        for i in range(count)
    ]
    return pl.pallas_call(
        functools.partial(core_kernel, s, keep_own),
        out_shape=out,
        in_specs=[VMEM] * (count + 1),
        out_specs=[VMEM] * count,
        compiler_params=pltpu.CompilerParams(vmem_limit_bytes=2**20),
    )(*keep, recv)


def final_kernel(s, n_dq, n_kv, *refs):
    dq, kv = refs[:n_dq], refs[n_dq : n_dq + n_kv]
    outs = refs[n_dq + n_kv :]
    r = s.rows
    for out, sources, base in ((outs[0], dq, 0), (outs[1], kv, 0), (outs[2], kv, s.part)):
        for t in range(s.tiles):
            rows = slice(base + t * r, base + (t + 1) * r)
            total = sources[0][rows, :].astype(F32)
            for ref in sources[1:]:
                total = total + ref[rows, :].astype(F32)
            out[:, t * LANES : (t + 1) * LANES] = total.astype(BF16)


def finish(s, dq, kv):
    return pl.pallas_call(
        functools.partial(final_kernel, s, len(dq), len(kv)),
        out_shape=[jax.ShapeDtypeStruct((s.rows, s.width), BF16)] * 3,
        in_specs=[VMEM] * (len(dq) + len(kv)),
        out_specs=[VMEM] * 3,
        compiler_params=pltpu.CompilerParams(vmem_limit_bytes=2**20),
    )(*dq, *kv)


def local(queries, keys, values, attended, grad_out, logsumexp):
    group, ctx = lax.axis_size("head"), lax.axis_size("ctx")
    s = Sizes(queries.shape[0], queries.shape[1], logsumexp.shape[1], group, ctx)

    def move(x, ctx_off, head_off):
        if ctx_off == 0:
            return lax.ppermute(x, "head", [(i, i ^ head_off) for i in range(group)])
        if head_off == 0:
            return lax.ppermute(x, "ctx", [(i, i ^ ctx_off) for i in range(ctx)])
        pairs = [
            (i * group + j, (i ^ ctx_off) * group + (j ^ head_off))
            for i in range(ctx)
            for j in range(group)
        ]
        return lax.ppermute(x, ("ctx", "head"), pairs)

    tie = lax.optimization_barrier
    qg_own, kv_own = pack(s, queries, keys, values, attended, grad_out, logsumexp)
    bits = [1 << i for i in reversed(range(s.high.bit_length() - 1))]
    far = {0: move(qg_own, s.high, 0)}
    kv = {0: kv_own}
    kv.update({bit: move(kv_own, bit, 0) for bit in bits})
    near = {0: qg_own, group // 2: move(qg_own, 0, group // 2)}
    for bit in bits:
        for off in sorted(off for off in kv if off % (2 * bit) == 0 and off):
            kv[off + bit] = move(kv[off], bit, 0)
    bit = group // 2
    while bit:
        for blocks in (far, near):
            for off in sorted(off for off in blocks if off % (2 * bit) == 0):
                if off + bit not in blocks and not (blocks is far and bit == 1 and off == group // 2):
                    blocks[off + bit] = move(blocks[off], 0, bit)
        bit //= 2
    kv = [kv[off] for off in range(s.high)]
    keep0, send0, sums0 = attend(s, [near[i] for i in range(group)], kv, None)
    keep0, send0, sums0, far = tie((keep0, send0, sums0, far))
    far[group // 2 + 1] = move(far[group // 2], 0, 1)
    keep1, send1, sums1 = attend(s, [far[i] for i in range(group)], kv, sums0[0])
    dq = core_add(s, keep0, move(send0, 0, 1), True)
    total_q = [dq[0]] + [move(dq[i], 0, 2 * i) for i in range(1, group // 2)]
    dq = core_add(s, keep1, move(send1, 0, 1), False)
    total_q += [move(dq[i], s.high, 2 * i) for i in range(group // 2)]
    total_kv = [sums1[0]] + [move(sums1[off], off, 0) for off in range(1, s.high)]
    return tuple(finish(s, total_q, total_kv))


def solution(mesh):
    rows = P(("ctx", "head"), None)
    return jax.shard_map(
        local,
        mesh=mesh,
        in_specs=(rows, rows, rows, rows, rows, P("ctx", "head")),
        out_specs=(rows, rows, rows),
        check_vma=False,
    )
```

```python
import functools
import jax
import jax.numpy as jnp
from jax import lax
from jax.experimental import pallas as pl
from jax.experimental.pallas import tpu as pltpu
from jax.sharding import PartitionSpec as P

F32 = jnp.float32
BF16 = jnp.bfloat16
LANES = 128
NT = (((1,), (1,)), ((), ()))
TN = (((0,), (0,)), ((), ()))
NN = (((1,), (0,)), ((), ()))
VMEM = pl.BlockSpec(memory_space=pltpu.VMEM)


def dot(a, b, dims):
    return lax.dot_general(a, b, dims, preferred_element_type=F32)


def round_up(n, m):
    return -(-n // m) * m


class Sizes:
    def __init__(self, rows, width, heads_group, group, ctx):
        self.rows, self.width = rows, width
        self.group, self.ctx = group, ctx
        self.heads_group = heads_group
        self.heads = heads_group * group
        self.dim = width // self.heads
        self.tiles = width // LANES
        self.span = rows * group
        self.span_tiles = -(-self.span // LANES)
        self.part = self.tiles * rows
        self.lse_rows = 3 * heads_group * self.span_tiles
        self.extra = round_up(self.lse_rows + 2 * self.heads, 16)
        self.high = ctx // 2

    def grant(self, blocks):
        scratch = 8 * self.tiles * self.span * LANES
        pairs = blocks * self.rows * round_up(self.span, LANES)
        return 2 * scratch + 32 * pairs + 2**20


def split3(x):
    hi = x.astype(BF16).astype(F32)
    rest = x - hi
    mid = rest.astype(BF16).astype(F32)
    return hi, mid, rest - mid


def pack_kernel(s, q_in, k_in, v_in, o_in, g_in, lse_in, qg_ref, kv_ref, *scratch):
    q_ref, k_ref, v_ref, o_ref, g_ref, lse_ref, small, sems = scratch
    copies = [
        pltpu.make_async_copy(source, target, sems.at[i])
        for i, (source, target) in enumerate(
            (
                (g_in, g_ref),
                (o_in, o_ref),
                (lse_in, lse_ref),
                (q_in, q_ref),
                (k_in, k_ref),
                (v_in, v_ref),
            )
        )
    ]
    for copy in copies:
        copy.start()
    r = s.rows
    copies[0].wait()
    copies[1].wait()
    prod = g_ref[...].astype(F32) * o_ref[...].astype(F32)
    hi = prod.astype(BF16)
    lo = (prod - hi.astype(F32)).astype(BF16)
    shape = (round_up(s.heads, 16), s.width)
    pick = lax.broadcasted_iota(jnp.int32, shape, 1) // s.dim
    pick = (pick == lax.broadcasted_iota(jnp.int32, shape, 0)).astype(F32).astype(BF16)
    delta = dot(pick, hi, NT) + dot(pick, lo, NT)
    d_hi, d_mid, _ = split3(delta)
    small[...] = jnp.zeros(small.shape, F32)
    copies[2].wait()
    h = s.heads_group
    at = 0
    for t in range(s.span_tiles):
        lanes = min(LANES, s.span - t * LANES)
        for piece in split3(lse_ref[:, t * LANES : t * LANES + lanes]):
            small[at : at + h, :lanes] = piece
            at += h
    small[at : at + s.heads, :r] = d_hi[: s.heads]
    small[at + s.heads : at + 2 * s.heads, :r] = d_mid[: s.heads]
    qg_ref[2 * s.part :, :] = small[...].astype(BF16)
    for copy in copies[3:]:
        copy.wait()
    for t in range(s.tiles):
        lanes = slice(t * LANES, (t + 1) * LANES)
        rows = slice(t * r, (t + 1) * r)
        more = slice(s.part + t * r, s.part + (t + 1) * r)
        qg_ref[rows, :] = q_ref[:, lanes]
        qg_ref[more, :] = g_ref[:, lanes]
        kv_ref[rows, :] = k_ref[:, lanes]
        kv_ref[more, :] = v_ref[:, lanes]


def in_hbm(x):
    return pltpu.with_memory_space_constraint(x, pltpu.HBM)


def pack(s, q, k, v, o, g, lse):
    return pl.pallas_call(
        functools.partial(pack_kernel, s),
        out_shape=(
            jax.ShapeDtypeStruct((2 * s.part + s.extra, LANES), BF16),
            jax.ShapeDtypeStruct((2 * s.part, LANES), BF16),
        ),
        in_specs=[pl.BlockSpec(memory_space=pl.ANY)] * 6,
        out_specs=[VMEM] * 2,
        scratch_shapes=[pltpu.VMEM((s.rows, s.width), BF16)] * 5
        + [
            pltpu.VMEM((s.heads_group, s.span), F32),
            pltpu.VMEM((s.extra, LANES), F32),
            pltpu.SemaphoreType.DMA((6,)),
        ],
        compiler_params=pltpu.CompilerParams(vmem_limit_bytes=2 * 2**20),
    )(*[in_hbm(x) for x in (q, k, v, o, g, jnp.transpose(lse))])


def attend_kernel(s, blocks, first, *refs):
    r, n = s.rows, s.group
    refs = list(refs)
    take = lambda count: [refs.pop(0) for _ in range(count)]
    qg, kv = take(n), take(blocks)
    (old,) = take(1) if not first else (None,)
    keep, (send,) = take(n // 2), take(1)
    sums = take(1 if first else blocks)
    qs, gs, dqs, norms, deltas = refs
    me = lax.axis_index("head")
    scale = s.dim**-0.5
    wide = s.span_tiles * LANES
    h = s.heads_group
    total = jnp.zeros((s.heads, wide), F32)
    for off in range(n):
        who = lax.bitwise_xor(me, off)
        at = pl.multiple_of(who * r, 16)
        for t in range(s.tiles):
            q = qg[off][t * r : (t + 1) * r, :]
            qs[t, pl.ds(at, r), :] = (q.astype(F32) * scale).astype(BF16)
            gs[t, pl.ds(at, r), :] = qg[off][s.part + t * r : s.part + (t + 1) * r, :]
        small = qg[off][2 * s.part :, :].astype(F32)
        pieces = []
        for t in range(s.span_tiles):
            b = 3 * h * t
            pieces.append(small[b : b + h] + small[b + h : b + 2 * h] + small[b + 2 * h : b + 3 * h])
        norms[who, :h, :] = jnp.concatenate(pieces, axis=1)
        b = s.lse_rows
        delta = small[b : b + s.heads] + small[b + s.heads : b + 2 * s.heads]
        if wide > LANES:
            delta = jnp.concatenate([delta, jnp.zeros((s.heads, wide - LANES), F32)], axis=1)
        total = total + pltpu.roll(delta, who * r, 1)
    deltas[...] = total
    size = blocks * r
    lane = lax.broadcasted_iota(jnp.int32, (2 * size, LANES), 1) < s.dim
    first_head = lax.broadcasted_iota(jnp.int32, (2 * size, LANES), 0) < size
    own_lanes = lane == first_head
    half = lane[:size]
    zero = jnp.zeros((), BF16)

    def pair(block):
        return jnp.where(own_lanes, jnp.concatenate([block, block], axis=0), zero)

    for t in range(s.tiles):
        rows = slice(t * r, (t + 1) * r)
        more = slice(s.part + t * r, s.part + (t + 1) * r)
        k = pair(jnp.concatenate([ref[rows, :] for ref in kv], axis=0))
        v = pair(jnp.concatenate([ref[more, :] for ref in kv], axis=0))
        q, g = qs[t], gs[t]
        scores = dot(k, q, NT)
        dweights = dot(v, g, NT)
        low, dscores = [], []
        for e in range(2):
            head = 2 * t + e
            mine = slice(e * size, (e + 1) * size)
            j = head % h
            weights = jnp.exp(scores[mine] - norms[head // h, j : j + 1, : s.span])
            low.append(weights.astype(BF16))
            gap = dweights[mine] - deltas[head : head + 1, : s.span]
            dscores.append((weights * gap).astype(BF16))
        low = jnp.concatenate(low, axis=0)
        dscores = jnp.concatenate(dscores, axis=0)
        dv = dot(low, g, NN)
        dk = dot(dscores, q, NN)
        dv, dk = [dv[:size], dv[size:]], [dk[:size], dk[size:]]
        dq = dot(dscores, k, TN)
        dqs[t] = dq * scale
        for where, parts in ((rows, dk), (more, dv)):
            both = jnp.where(half, parts[0], parts[1])
            for i in range(blocks):
                piece = both[i * r : (i + 1) * r]
                if first:
                    sums[0][2 * s.part * i + where.start : 2 * s.part * i + where.stop, :] = piece
                else:
                    piece = piece + old[2 * s.part * i + where.start : 2 * s.part * i + where.stop, :]
                    sums[i][where, :] = piece.astype(sums[i].dtype)
    for off in range(n):
        at = pl.multiple_of(lax.bitwise_xor(me, off) * r, 16)
        for t in range(s.tiles):
            piece = dqs[t, pl.ds(at, r), :]
            i = off // 2
            if off % 2 == 0:
                keep[i][t * r : (t + 1) * r, :] = piece
            else:
                send[i * s.part + t * r : i * s.part + (t + 1) * r, :] = piece.astype(BF16)


def attend(s, qg, kv, old):
    blocks = len(kv)
    first = old is None
    out = [jax.ShapeDtypeStruct((s.part, LANES), F32)] * (s.group // 2)
    out.append(jax.ShapeDtypeStruct((s.group // 2 * s.part, LANES), BF16))
    if first:
        out.append(jax.ShapeDtypeStruct((blocks * 2 * s.part, LANES), F32))
    else:
        out += [
            jax.ShapeDtypeStruct((2 * s.part, LANES), BF16 if i % 2 else F32)
            for i in range(blocks)
        ]
    operands = list(qg) + list(kv) + ([] if first else [old])
    pairs = s.heads * s.span * blocks * s.rows
    result = pl.pallas_call(
        functools.partial(attend_kernel, s, blocks, first),
        out_shape=out,
        in_specs=[VMEM] * len(operands),
        out_specs=[VMEM] * len(out),
        scratch_shapes=[
            pltpu.VMEM((s.tiles, s.span, LANES), BF16),
            pltpu.VMEM((s.tiles, s.span, LANES), BF16),
            pltpu.VMEM((s.tiles, s.span, LANES), F32),
            pltpu.VMEM((s.group, 8, s.span_tiles * LANES), F32),
            pltpu.VMEM((s.heads, s.span_tiles * LANES), F32),
        ],
        compiler_params=pltpu.CompilerParams(vmem_limit_bytes=s.grant(blocks)),
        cost_estimate=pl.CostEstimate(
            flops=20 * pairs * s.dim, bytes_accessed=4 * s.part * LANES * 8, transcendentals=pairs
        ),
    )(*operands)
    count = s.group // 2
    return result[:count], result[count], result[count + 1 :]


def core_kernel(s, keep_own, *refs):
    count = s.group // 2
    recv = refs[count]
    for i in range(count):
        total = refs[i][...] + recv[i * s.part : (i + 1) * s.part, :].astype(F32)
        refs[count + 1 + i][...] = total.astype(refs[count + 1 + i].dtype)


def core_add(s, keep, recv, keep_own):
    count = len(keep)
    out = [
        jax.ShapeDtypeStruct((s.part, LANES), F32 if keep_own and i == 0 else BF16)
        for i in range(count)
    ]
    return pl.pallas_call(
        functools.partial(core_kernel, s, keep_own),
        out_shape=out,
        in_specs=[VMEM] * (count + 1),
        out_specs=[VMEM] * count,
        compiler_params=pltpu.CompilerParams(vmem_limit_bytes=2**20),
    )(*keep, recv)


def sum_kernel(*refs):
    total = refs[0][...].astype(F32)
    for ref in refs[1:-1]:
        total = total + ref[...].astype(F32)
    refs[-1][...] = total.astype(refs[-1].dtype)


def sum_low(arrays):
    if len(arrays) == 1:
        return arrays[0] if arrays[0].dtype == BF16 else arrays[0].astype(BF16)
    return pl.pallas_call(
        sum_kernel,
        out_shape=jax.ShapeDtypeStruct(arrays[0].shape, BF16),
        in_specs=[VMEM] * len(arrays),
        out_specs=VMEM,
        compiler_params=pltpu.CompilerParams(vmem_limit_bytes=2**20),
    )(*arrays)


def sum_all(s, arrays):
    return pl.pallas_call(
        sum_kernel,
        out_shape=jax.ShapeDtypeStruct(arrays[0].shape, F32),
        in_specs=[VMEM] * len(arrays),
        out_specs=VMEM,
        compiler_params=pltpu.CompilerParams(vmem_limit_bytes=2**20),
        cost_estimate=pl.CostEstimate(flops=10**10, bytes_accessed=0, transcendentals=0),
    )(*arrays)


def final_kernel(s, count, *refs):
    dq, kv, outs = refs[0], refs[1 : count + 1], refs[count + 1 :]
    r = s.rows
    for out, sources, base in ((outs[0], [dq], 0), (outs[1], kv, 0), (outs[2], kv, s.part)):
        for t in range(s.tiles):
            rows = slice(base + t * r, base + (t + 1) * r)
            total = sources[0][rows, :].astype(F32)
            for ref in sources[1:]:
                total = total + ref[rows, :].astype(F32)
            out[:, t * LANES : (t + 1) * LANES] = total.astype(BF16)


def finish(s, dq, kv):
    return pl.pallas_call(
        functools.partial(final_kernel, s, len(kv)),
        out_shape=[jax.ShapeDtypeStruct((s.rows, s.width), BF16)] * 3,
        in_specs=[VMEM] * (len(kv) + 1),
        out_specs=[VMEM] * 3,
        compiler_params=pltpu.CompilerParams(vmem_limit_bytes=2**20),
    )(dq, *kv)


def local(queries, keys, values, attended, grad_out, logsumexp):
    group, ctx = lax.axis_size("head"), lax.axis_size("ctx")
    s = Sizes(queries.shape[0], queries.shape[1], logsumexp.shape[1], group, ctx)

    def move(x, ctx_off, head_off):
        if ctx_off == 0:
            return lax.ppermute(x, "head", [(i, i ^ head_off) for i in range(group)])
        if head_off == 0:
            return lax.ppermute(x, "ctx", [(i, i ^ ctx_off) for i in range(ctx)])
        pairs = [
            (i * group + j, (i ^ ctx_off) * group + (j ^ head_off))
            for i in range(ctx)
            for j in range(group)
        ]
        return lax.ppermute(x, ("ctx", "head"), pairs)

    tie = lax.optimization_barrier
    qg_own, kv_own = pack(s, queries, keys, values, attended, grad_out, logsumexp)
    bits = [1 << i for i in reversed(range(s.high.bit_length() - 1))]
    far = {0: move(qg_own, s.high, 0)}
    kv = {0: kv_own}
    kv.update({bit: move(kv_own, bit, 0) for bit in bits})
    near = {0: qg_own, group // 2: move(qg_own, 0, group // 2)}
    for bit in bits:
        for off in sorted(off for off in kv if off % (2 * bit) == 0 and off):
            kv[off + bit] = move(kv[off], bit, 0)
    bit = group // 2
    while bit:
        for blocks in (far, near):
            for off in sorted(off for off in blocks if off % (2 * bit) == 0):
                if off + bit not in blocks and not (blocks is far and bit == 1 and off == group // 2):
                    blocks[off + bit] = move(blocks[off], 0, bit)
        bit //= 2
    kv = [kv[off] for off in range(s.high)]
    keep0, send0, sums0 = attend(s, [near[i] for i in range(group)], kv, None)
    keep0, send0, sums0, far = tie((keep0, send0, sums0, far))
    far[group // 2 + 1] = move(far[group // 2], 0, 1)
    keep1, send1, sums1 = attend(s, [far[i] for i in range(group)], kv, sums0[0])
    dq = core_add(s, keep1, move(send1, 0, 1), False)
    total_q = [move(dq[i], s.high, 2 * i) for i in range(group // 2)]
    dq = core_add(s, keep0, move(send0, 0, 1), True)
    total_q += [dq[0]] + [move(dq[i], 0, 2 * i) for i in range(1, group // 2)]
    parts = {off: [sums1[off]] for off in range(s.high)}
    for bit in reversed(bits):
        others = [off for off in range(s.high) if off & (2 * bit - 1) == bit and off != bit]
        for off in others:
            parts[off - bit].append(move(sum_low(parts[off]), bit, 0))
        last = sum_low(parts[bit])
        if others:
            last, parts[others[0] - bit] = tie((last, parts[others[0] - bit]))
        parts[0].append(move(last, bit, 0))
    total_q = sum_all(s, total_q)
    return tuple(finish(s, total_q, parts[0]))


def solution(mesh):
    rows = P(("ctx", "head"), None)
    return jax.shard_map(
        local,
        mesh=mesh,
        in_specs=(rows, rows, rows, rows, rows, P("ctx", "head")),
        out_specs=(rows, rows, rows),
        check_vma=False,
    )
```

```python
import functools
import jax
import jax.numpy as jnp
from jax import lax
from jax.experimental import pallas as pl
from jax.experimental.pallas import tpu as pltpu
from jax.sharding import PartitionSpec as P

F32 = jnp.float32
BF16 = jnp.bfloat16
LANES = 128
NT = (((1,), (1,)), ((), ()))
TN = (((0,), (0,)), ((), ()))
NN = (((1,), (0,)), ((), ()))
VMEM = pl.BlockSpec(memory_space=pltpu.VMEM)


def dot(a, b, dims):
    return lax.dot_general(a, b, dims, preferred_element_type=F32)


def round_up(n, m):
    return -(-n // m) * m


class Sizes:
    def __init__(self, rows, width, heads_group, group, ctx):
        self.rows, self.width = rows, width
        self.group, self.ctx = group, ctx
        self.heads_group = heads_group
        self.heads = heads_group * group
        self.dim = width // self.heads
        self.tiles = width // LANES
        self.span = rows * group
        self.span_tiles = -(-self.span // LANES)
        self.part = self.tiles * rows
        self.lse_rows = 2 * heads_group * self.span_tiles
        self.extra = round_up(self.lse_rows + self.heads, 16)
        self.high = ctx // 2

    def grant(self, blocks):
        scratch = 8 * self.tiles * self.span * LANES
        pairs = blocks * self.rows * round_up(self.span, LANES)
        return 2 * scratch + 32 * pairs + 2**20


def split2(x):
    hi = x.astype(BF16).astype(F32)
    return hi, x - hi


def pack_kernel(s, q_in, k_in, v_in, o_in, g_in, lse_in, qg_ref, kv_ref, *scratch):
    q_ref, k_ref, v_ref, o_ref, g_ref, lse_ref, small, side, sems = scratch
    copies = [
        pltpu.make_async_copy(source, target, sems.at[i])
        for i, (source, target) in enumerate(
            (
                (g_in, g_ref),
                (o_in, o_ref),
                (lse_in, lse_ref),
                (q_in, q_ref),
                (k_in, k_ref),
                (v_in, v_ref),
            )
        )
    ]
    for copy in copies:
        copy.start()
    r = s.rows
    copies[0].wait()
    copies[1].wait()
    prod = g_ref[...].astype(F32) * o_ref[...].astype(F32)
    hi = prod.astype(BF16)
    lo = (prod - hi.astype(F32)).astype(BF16)
    shape = (round_up(s.heads, 16), s.width)
    pick = lax.broadcasted_iota(jnp.int32, shape, 1) // s.dim
    pick = (pick == lax.broadcasted_iota(jnp.int32, shape, 0)).astype(F32).astype(BF16)
    delta = dot(pick, hi, NT) + dot(pick, lo, NT)
    d_hi, d_low = split2(delta)
    small[...] = jnp.zeros(small.shape, F32)
    side[...] = jnp.zeros(side.shape, F32)
    side[:, :r] = d_low
    d_low = pltpu.roll(side[...], LANES // 2, 1)
    side[:, :r] = d_hi
    deltas = side[...] + d_low
    copies[2].wait()
    h = s.heads_group
    at = 0
    for t in range(s.span_tiles):
        lanes = min(LANES, s.span - t * LANES)
        for piece in split2(lse_ref[:, t * LANES : t * LANES + lanes]):
            small[at : at + h, :lanes] = piece
            at += h
    small[at : at + s.heads, :] = deltas[: s.heads]
    qg_ref[2 * s.part :, :] = small[...].astype(BF16)
    for copy in copies[3:]:
        copy.wait()
    for t in range(s.tiles):
        lanes = slice(t * LANES, (t + 1) * LANES)
        rows = slice(t * r, (t + 1) * r)
        more = slice(s.part + t * r, s.part + (t + 1) * r)
        qg_ref[rows, :] = q_ref[:, lanes]
        qg_ref[more, :] = g_ref[:, lanes]
        kv_ref[rows, :] = k_ref[:, lanes]
        kv_ref[more, :] = v_ref[:, lanes]


def in_hbm(x):
    return pltpu.with_memory_space_constraint(x, pltpu.HBM)


def pack(s, q, k, v, o, g, lse):
    return pl.pallas_call(
        functools.partial(pack_kernel, s),
        out_shape=(
            jax.ShapeDtypeStruct((2 * s.part + s.extra, LANES), BF16),
            jax.ShapeDtypeStruct((2 * s.part, LANES), BF16),
        ),
        in_specs=[pl.BlockSpec(memory_space=pl.ANY)] * 6,
        out_specs=[VMEM] * 2,
        scratch_shapes=[pltpu.VMEM((s.rows, s.width), BF16)] * 5
        + [
            pltpu.VMEM((s.heads_group, s.span), F32),
            pltpu.VMEM((s.extra, LANES), F32),
            pltpu.VMEM((round_up(s.heads, 16), LANES), F32),
            pltpu.SemaphoreType.DMA((6,)),
        ],
        compiler_params=pltpu.CompilerParams(vmem_limit_bytes=2 * 2**20),
    )(*[in_hbm(x) for x in (q, k, v, o, g, jnp.transpose(lse))])


def attend_kernel(s, blocks, first, *refs):
    r, n = s.rows, s.group
    refs = list(refs)
    take = lambda count: [refs.pop(0) for _ in range(count)]
    qg, kv = take(n), take(blocks)
    (old,) = take(1) if not first else (None,)
    keep, (send,) = take(n // 2), take(1)
    sums = take(1 if first else blocks)
    qs, gs, dqs, norms, deltas = refs
    me = lax.axis_index("head")
    scale = s.dim**-0.5
    wide = s.span_tiles * LANES
    h = s.heads_group
    total = jnp.zeros((s.heads, wide), F32)
    used = lax.broadcasted_iota(jnp.int32, (s.heads, LANES), 1) < r
    for off in range(n):
        who = lax.bitwise_xor(me, off)
        at = pl.multiple_of(who * r, 16)
        for t in range(s.tiles):
            q = qg[off][t * r : (t + 1) * r, :]
            qs[t, pl.ds(at, r), :] = (q.astype(F32) * scale).astype(BF16)
            gs[t, pl.ds(at, r), :] = qg[off][s.part + t * r : s.part + (t + 1) * r, :]
        small = qg[off][2 * s.part :, :].astype(F32)
        pieces = []
        for t in range(s.span_tiles):
            b = 2 * h * t
            pieces.append(small[b : b + h] + small[b + h : b + 2 * h])
        norms[who, :h, :] = jnp.concatenate(pieces, axis=1)
        b = s.lse_rows
        delta = small[b : b + s.heads]
        delta = jnp.where(used, delta + pltpu.roll(delta, LANES // 2, 1), 0.0)
        if wide > LANES:
            delta = jnp.concatenate([delta, jnp.zeros((s.heads, wide - LANES), F32)], axis=1)
        total = total + pltpu.roll(delta, who * r, 1)
    deltas[...] = total
    size = blocks * r
    lane = lax.broadcasted_iota(jnp.int32, (2 * size, LANES), 1) < s.dim
    first_head = lax.broadcasted_iota(jnp.int32, (2 * size, LANES), 0) < size
    own_lanes = lane == first_head
    half = lane[:size]
    zero = jnp.zeros((), BF16)

    def pair(block):
        return jnp.where(own_lanes, jnp.concatenate([block, block], axis=0), zero)

    def front(t):
        rows = slice(t * r, (t + 1) * r)
        more = slice(s.part + t * r, s.part + (t + 1) * r)
        k = pair(jnp.concatenate([ref[rows, :] for ref in kv], axis=0))
        v = pair(jnp.concatenate([ref[more, :] for ref in kv], axis=0))
        return k, dot(k, qs[t], NT), dot(v, gs[t], NT)

    def middle(t, scores, dweights):
        low, dscores = [], []
        for e in range(2):
            head = 2 * t + e
            mine = slice(e * size, (e + 1) * size)
            j = head % h
            weights = jnp.exp(scores[mine] - norms[head // h, j : j + 1, : s.span])
            low.append(weights.astype(BF16))
            gap = dweights[mine] - deltas[head : head + 1, : s.span]
            dscores.append((weights * gap).astype(BF16))
        return jnp.concatenate(low, axis=0), jnp.concatenate(dscores, axis=0)

    def back(t, k, low, dscores):
        rows = slice(t * r, (t + 1) * r)
        more = slice(s.part + t * r, s.part + (t + 1) * r)
        dv = dot(low, gs[t], NN)
        dk = dot(dscores, qs[t], NN)
        dv, dk = [dv[:size], dv[size:]], [dk[:size], dk[size:]]
        dqs[t] = dot(k, dscores, TN).T * scale
        for where, parts in ((rows, dk), (more, dv)):
            both = jnp.where(half, parts[0], parts[1])
            for i in range(blocks):
                piece = both[i * r : (i + 1) * r]
                if first:
                    sums[0][2 * s.part * i + where.start : 2 * s.part * i + where.stop, :] = piece
                else:
                    piece = piece + old[2 * s.part * i + where.start : 2 * s.part * i + where.stop, :]
                    sums[i][where, :] = piece.astype(sums[i].dtype)

    ahead = front(0)
    for t in range(s.tiles):
        k, scores, dweights = ahead
        if t + 1 < s.tiles:
            ahead = front(t + 1)
        back(t, k, *middle(t, scores, dweights))
    for off in range(n):
        at = pl.multiple_of(lax.bitwise_xor(me, off) * r, 16)
        for t in range(s.tiles):
            piece = dqs[t, pl.ds(at, r), :]
            i = off // 2
            if off % 2 == 0:
                keep[i][t * r : (t + 1) * r, :] = piece
            else:
                send[i * s.part + t * r : i * s.part + (t + 1) * r, :] = piece.astype(BF16)


def attend(s, qg, kv, old):
    blocks = len(kv)
    first = old is None
    out = [jax.ShapeDtypeStruct((s.part, LANES), F32)] * (s.group // 2)
    out.append(jax.ShapeDtypeStruct((s.group // 2 * s.part, LANES), BF16))
    if first:
        out.append(jax.ShapeDtypeStruct((blocks * 2 * s.part, LANES), F32))
    else:
        out += [
            jax.ShapeDtypeStruct((2 * s.part, LANES), BF16 if i % 2 else F32)
            for i in range(blocks)
        ]
    operands = list(qg) + list(kv) + ([] if first else [old])
    pairs = s.heads * s.span * blocks * s.rows
    result = pl.pallas_call(
        functools.partial(attend_kernel, s, blocks, first),
        out_shape=out,
        in_specs=[VMEM] * len(operands),
        out_specs=[VMEM] * len(out),
        scratch_shapes=[
            pltpu.VMEM((s.tiles, s.span, LANES), BF16),
            pltpu.VMEM((s.tiles, s.span, LANES), BF16),
            pltpu.VMEM((s.tiles, s.span, LANES), F32),
            pltpu.VMEM((s.group, 8, s.span_tiles * LANES), F32),
            pltpu.VMEM((s.heads, s.span_tiles * LANES), F32),
        ],
        compiler_params=pltpu.CompilerParams(vmem_limit_bytes=s.grant(blocks)),
        cost_estimate=pl.CostEstimate(
            flops=(20 if first else 200) * pairs * s.dim, bytes_accessed=4 * s.part * LANES * 8, transcendentals=pairs
        ),
    )(*operands)
    count = s.group // 2
    return result[:count], result[count], result[count + 1 :]


def core_kernel(s, keep_own, *refs):
    count = s.group // 2
    recv = refs[count]
    for i in range(count):
        total = refs[i][...] + recv[i * s.part : (i + 1) * s.part, :].astype(F32)
        refs[count + 1 + i][...] = total.astype(refs[count + 1 + i].dtype)


def core_add(s, keep, recv, keep_own):
    count = len(keep)
    out = [
        jax.ShapeDtypeStruct((s.part, LANES), F32 if keep_own and i == 0 else BF16)
        for i in range(count)
    ]
    return pl.pallas_call(
        functools.partial(core_kernel, s, keep_own),
        out_shape=out,
        in_specs=[VMEM] * (count + 1),
        out_specs=[VMEM] * count,
        compiler_params=pltpu.CompilerParams(vmem_limit_bytes=2**20),
    )(*keep, recv)


def sum_kernel(*refs):
    total = refs[0][...].astype(F32)
    for ref in refs[1:-1]:
        total = total + ref[...].astype(F32)
    refs[-1][...] = total.astype(refs[-1].dtype)


def sum_low(arrays):
    if len(arrays) == 1:
        return arrays[0] if arrays[0].dtype == BF16 else arrays[0].astype(BF16)
    return pl.pallas_call(
        sum_kernel,
        out_shape=jax.ShapeDtypeStruct(arrays[0].shape, BF16),
        in_specs=[VMEM] * len(arrays),
        out_specs=VMEM,
        compiler_params=pltpu.CompilerParams(vmem_limit_bytes=2**20),
    )(*arrays)


def sum_all(s, arrays):
    return pl.pallas_call(
        sum_kernel,
        out_shape=jax.ShapeDtypeStruct(arrays[0].shape, F32),
        in_specs=[VMEM] * len(arrays),
        out_specs=VMEM,
        compiler_params=pltpu.CompilerParams(vmem_limit_bytes=2**20),
        cost_estimate=pl.CostEstimate(flops=4000000000, bytes_accessed=0, transcendentals=0),
    )(*arrays)


def final_kernel(s, n_dq, n_kv, *refs):
    dq, kv, outs = refs[:n_dq], refs[n_dq : n_dq + n_kv], refs[n_dq + n_kv :]
    r = s.rows
    for out, sources, base in ((outs[0], dq, 0), (outs[1], kv, 0), (outs[2], kv, s.part)):
        for t in range(s.tiles):
            rows = slice(base + t * r, base + (t + 1) * r)
            total = sources[0][rows, :].astype(F32)
            for ref in sources[1:]:
                total = total + ref[rows, :].astype(F32)
            out[:, t * LANES : (t + 1) * LANES] = total.astype(BF16)


def finish(s, dq, kv):
    return pl.pallas_call(
        functools.partial(final_kernel, s, len(dq), len(kv)),
        out_shape=[jax.ShapeDtypeStruct((s.rows, s.width), BF16)] * 3,
        in_specs=[VMEM] * (len(dq) + len(kv)),
        out_specs=[VMEM] * 3,
        compiler_params=pltpu.CompilerParams(vmem_limit_bytes=2**20),
    )(*dq, *kv)


def hold(x, flops):
    return pl.pallas_call(
        lambda ref, out: None,
        out_shape=jax.ShapeDtypeStruct(x.shape, x.dtype),
        in_specs=[VMEM],
        out_specs=VMEM,
        input_output_aliases={0: 0},
        compiler_params=pltpu.CompilerParams(vmem_limit_bytes=2**20),
        cost_estimate=pl.CostEstimate(flops=flops, bytes_accessed=0, transcendentals=0),
    )(x)


def local(queries, keys, values, attended, grad_out, logsumexp):
    group, ctx = lax.axis_size("head"), lax.axis_size("ctx")
    s = Sizes(queries.shape[0], queries.shape[1], logsumexp.shape[1], group, ctx)

    def move(x, ctx_off, head_off):
        if ctx_off == 0:
            return lax.ppermute(x, "head", [(i, i ^ head_off) for i in range(group)])
        if head_off == 0:
            return lax.ppermute(x, "ctx", [(i, i ^ ctx_off) for i in range(ctx)])
        pairs = [
            (i * group + j, (i ^ ctx_off) * group + (j ^ head_off))
            for i in range(ctx)
            for j in range(group)
        ]
        return lax.ppermute(x, ("ctx", "head"), pairs)

    tie = lax.optimization_barrier
    qg_own, kv_own = pack(s, queries, keys, values, attended, grad_out, logsumexp)
    bits = [1 << i for i in reversed(range(s.high.bit_length() - 1))]
    side = group // 2
    far, kv, near = {}, {0: kv_own}, {0: qg_own}
    far[0] = move(qg_own, s.high, 0)
    kv[bits[0]] = move(kv_own, bits[0], 0)
    kv.update({bit: move(kv_own, bit, 0) for bit in bits[1:]})
    near[side] = move(qg_own, 0, side)
    kv[bits[0]] = hold(kv[bits[0]], 10000000000)
    for bit in bits:
        for off in sorted(off for off in kv if off % (2 * bit) == 0 and off):
            kv[off + bit] = move(kv[off], bit, 0)
    far[side] = move(far[0], 0, side)
    kv[s.high - 1] = hold(kv[s.high - 1], 3000000000)
    bit = side
    while bit:
        for blocks in (far, near):
            for off in sorted(off for off in blocks if off % (2 * bit) == 0):
                if off + bit not in blocks and not (blocks is far and bit == 1 and off == side):
                    blocks[off + bit] = move(blocks[off], 0, bit)
        bit //= 2
    kv = [kv[off] for off in range(s.high)]
    keep0, send0, sums0 = attend(s, [near[i] for i in range(group)], kv, None)
    keep0, send0, sums0, far = tie((keep0, send0, sums0, far))
    far[side + 1] = move(far[side], 0, 1)
    keep1, send1, sums1 = attend(s, [far[i] for i in range(group)], kv, sums0[0])
    sums1 = list(sums1)
    dq = core_add(s, keep1, move(send1, 0, 1), False)
    total_q = [move(dq[i], s.high, 2 * i) for i in range(side)]
    dq = core_add(s, keep0, move(send0, 0, 1), True)
    late_q = [move(dq[i], 0, 2 * i) for i in range(1, side)]
    late_q = total_q[1:] + late_q
    total_q = total_q[:1]
    total_q = [dq[0]] + total_q
    parts = {off: [sums1[off]] for off in range(s.high)}
    for bit in reversed(bits):
        others = [off for off in range(s.high) if off & (2 * bit - 1) == bit and off != bit]
        for off in others:
            parts[off - bit].append(move(sum_low(parts[off]), bit, 0))
        parts[0].append(move(sum_low(parts[bit]), bit, 0))
    total_q = sum_all(s, total_q)
    return tuple(finish(s, [total_q] + late_q, parts[0]))


def solution(mesh):
    rows = P(("ctx", "head"), None)
    return jax.shard_map(
        local,
        mesh=mesh,
        in_specs=(rows, rows, rows, rows, rows, P("ctx", "head")),
        out_specs=(rows, rows, rows),
        check_vma=False,
    )
```

```python
import functools
import jax
import jax.numpy as jnp
from jax import lax
from jax.experimental import pallas as pl
from jax.experimental.pallas import tpu as pltpu
from jax.sharding import PartitionSpec as P

F32 = jnp.float32
BF16 = jnp.bfloat16
LANES = 128
NT = (((1,), (1,)), ((), ()))
TN = (((0,), (0,)), ((), ()))
NN = (((1,), (0,)), ((), ()))
VMEM = pl.BlockSpec(memory_space=pltpu.VMEM)


def dot(a, b, dims):
    return lax.dot_general(a, b, dims, preferred_element_type=F32)


def round_up(n, m):
    return -(-n // m) * m


class Sizes:
    def __init__(self, rows, width, heads_group, group, ctx):
        self.rows, self.width = rows, width
        self.group, self.ctx = group, ctx
        self.heads_group = heads_group
        self.heads = heads_group * group
        self.dim = width // self.heads
        self.tiles = width // LANES
        self.span = rows * group
        self.span_tiles = -(-self.span // LANES)
        self.part = self.tiles * rows
        self.lse_rows = 2 * heads_group * self.span_tiles
        self.extra = round_up(self.lse_rows + self.heads, 16)
        self.high = ctx // 2

    def grant(self, blocks):
        scratch = 8 * self.tiles * self.span * LANES
        pairs = blocks * self.rows * round_up(self.span, LANES)
        return 2 * scratch + 48 * pairs + 2**20


def split2(x):
    hi = x.astype(BF16).astype(F32)
    return hi, x - hi


def pack_kernel(s, q_in, k_in, v_in, o_in, g_in, lse_in, qg_ref, kv_ref, *scratch):
    q_ref, k_ref, v_ref, o_ref, g_ref, lse_ref, small, side, sems = scratch
    copies = [
        pltpu.make_async_copy(source, target, sems.at[i])
        for i, (source, target) in enumerate(
            (
                (g_in, g_ref),
                (o_in, o_ref),
                (lse_in, lse_ref),
                (q_in, q_ref),
                (k_in, k_ref),
                (v_in, v_ref),
            )
        )
    ]
    for copy in copies:
        copy.start()
    r = s.rows
    copies[0].wait()
    copies[1].wait()
    prod = g_ref[...].astype(F32) * o_ref[...].astype(F32)
    hi = prod.astype(BF16)
    lo = (prod - hi.astype(F32)).astype(BF16)
    shape = (round_up(s.heads, 16), s.width)
    pick = lax.broadcasted_iota(jnp.int32, shape, 1) // s.dim
    pick = (pick == lax.broadcasted_iota(jnp.int32, shape, 0)).astype(F32).astype(BF16)
    delta = dot(pick, hi, NT) + dot(pick, lo, NT)
    d_hi, d_low = split2(delta)
    small[...] = jnp.zeros(small.shape, F32)
    side[...] = jnp.zeros(side.shape, F32)
    side[:, :r] = d_low
    d_low = pltpu.roll(side[...], LANES // 2, 1)
    side[:, :r] = d_hi
    deltas = side[...] + d_low
    copies[2].wait()
    h = s.heads_group
    at = 0
    for t in range(s.span_tiles):
        lanes = min(LANES, s.span - t * LANES)
        for piece in split2(lse_ref[:, t * LANES : t * LANES + lanes]):
            small[at : at + h, :lanes] = piece
            at += h
    small[at : at + s.heads, :] = deltas[: s.heads]
    qg_ref[2 * s.part :, :] = small[...].astype(BF16)
    for copy in copies[3:]:
        copy.wait()
    for t in range(s.tiles):
        lanes = slice(t * LANES, (t + 1) * LANES)
        rows = slice(t * r, (t + 1) * r)
        more = slice(s.part + t * r, s.part + (t + 1) * r)
        qg_ref[rows, :] = (q_ref[:, lanes].astype(F32) * s.dim**-0.5).astype(BF16)
        qg_ref[more, :] = g_ref[:, lanes]
        kv_ref[rows, :] = k_ref[:, lanes]
        kv_ref[more, :] = v_ref[:, lanes]


def in_hbm(x):
    return pltpu.with_memory_space_constraint(x, pltpu.HBM)


def pack(s, q, k, v, o, g, lse):
    return pl.pallas_call(
        functools.partial(pack_kernel, s),
        out_shape=(
            jax.ShapeDtypeStruct((2 * s.part + s.extra, LANES), BF16),
            jax.ShapeDtypeStruct((2 * s.part, LANES), BF16),
        ),
        in_specs=[pl.BlockSpec(memory_space=pl.ANY)] * 6,
        out_specs=[VMEM] * 2,
        scratch_shapes=[pltpu.VMEM((s.rows, s.width), BF16)] * 5
        + [
            pltpu.VMEM((s.heads_group, s.span), F32),
            pltpu.VMEM((s.extra, LANES), F32),
            pltpu.VMEM((round_up(s.heads, 16), LANES), F32),
            pltpu.SemaphoreType.DMA((6,)),
        ],
        compiler_params=pltpu.CompilerParams(vmem_limit_bytes=2 * 2**20),
    )(*[in_hbm(x) for x in (q, k, v, o, g, jnp.transpose(lse))])


def attend_kernel(s, blocks, first, *refs):
    r, n = s.rows, s.group
    refs = list(refs)
    take = lambda count: [refs.pop(0) for _ in range(count)]
    qg, kv = take(n), take(blocks)
    (old,) = take(1) if not first else (None,)
    keep, (send,) = take(n // 2), take(1)
    sums = take(1 if first else blocks)
    qs, gs, dqs, norms, deltas = refs
    me = lax.axis_index("head")
    scale = s.dim**-0.5
    wide = s.span_tiles * LANES
    h = s.heads_group
    total = jnp.zeros((s.heads, wide), F32)
    used = lax.broadcasted_iota(jnp.int32, (s.heads, LANES), 1) < r
    for off in range(n):
        who = lax.bitwise_xor(me, off)
        at = pl.multiple_of(who * r, 16)
        for t in range(s.tiles):
            qs[t, pl.ds(at, r), :] = qg[off][t * r : (t + 1) * r, :]
            gs[t, pl.ds(at, r), :] = qg[off][s.part + t * r : s.part + (t + 1) * r, :]
        small = qg[off][2 * s.part :, :].astype(F32)
        pieces = []
        for t in range(s.span_tiles):
            b = 2 * h * t
            pieces.append(small[b : b + h] + small[b + h : b + 2 * h])
        norms[who, :h, :] = jnp.concatenate(pieces, axis=1)
        b = s.lse_rows
        delta = small[b : b + s.heads]
        delta = jnp.where(used, delta + pltpu.roll(delta, LANES // 2, 1), 0.0)
        if wide > LANES:
            delta = jnp.concatenate([delta, jnp.zeros((s.heads, wide - LANES), F32)], axis=1)
        total = total + pltpu.roll(delta, who * r, 1)
    deltas[...] = total
    size = blocks * r
    lane = lax.broadcasted_iota(jnp.int32, (2 * size, LANES), 1) < s.dim
    first_head = lax.broadcasted_iota(jnp.int32, (2 * size, LANES), 0) < size
    own_lanes = lane == first_head
    half = lane[:size]
    zero = jnp.zeros((), BF16)

    def pair(block):
        return jnp.where(own_lanes, jnp.concatenate([block, block], axis=0), zero)

    def front(t):
        rows = slice(t * r, (t + 1) * r)
        more = slice(s.part + t * r, s.part + (t + 1) * r)
        k = pair(jnp.concatenate([ref[rows, :] for ref in kv], axis=0))
        v = pair(jnp.concatenate([ref[more, :] for ref in kv], axis=0))
        return k, dot(k, qs[t], NT), dot(v, gs[t], NT)

    def middle(t, scores, dweights):
        low, dscores = [], []
        for e in range(2):
            head = 2 * t + e
            mine = slice(e * size, (e + 1) * size)
            j = head % h
            weights = jnp.exp(scores[mine] - norms[head // h, j : j + 1, : s.span])
            low.append(weights.astype(BF16))
            gap = dweights[mine] - deltas[head : head + 1, : s.span]
            dscores.append((weights * gap).astype(BF16))
        return jnp.concatenate(low, axis=0), jnp.concatenate(dscores, axis=0)

    def back(t, k, low, dscores):
        rows = slice(t * r, (t + 1) * r)
        more = slice(s.part + t * r, s.part + (t + 1) * r)
        dv = dot(low, gs[t], NN)
        dk = dot(dscores, qs[t], NN)
        dv, dk = [dv[:size], dv[size:]], [dk[:size], dk[size:]]
        dqs[t] = dot(k, dscores, TN).T * scale
        for where, parts in ((rows, dk), (more, dv)):
            both = jnp.where(half, parts[0], parts[1])
            for i in range(blocks):
                piece = both[i * r : (i + 1) * r]
                if first:
                    sums[0][2 * s.part * i + where.start : 2 * s.part * i + where.stop, :] = piece
                else:
                    piece = piece + old[2 * s.part * i + where.start : 2 * s.part * i + where.stop, :]
                    sums[i][where, :] = piece.astype(sums[i].dtype)

    ahead = [front(t) for t in range(min(2, s.tiles))]
    for t in range(s.tiles):
        k, scores, dweights = ahead.pop(0)
        if t + 2 < s.tiles:
            ahead.append(front(t + 2))
        back(t, k, *middle(t, scores, dweights))
    for off in range(n):
        at = pl.multiple_of(lax.bitwise_xor(me, off) * r, 16)
        for t in range(s.tiles):
            piece = dqs[t, pl.ds(at, r), :]
            i = off // 2
            if off % 2 == 0:
                keep[i][t * r : (t + 1) * r, :] = piece
            else:
                send[i * s.part + t * r : i * s.part + (t + 1) * r, :] = piece.astype(BF16)


def attend(s, qg, kv, old):
    blocks = len(kv)
    first = old is None
    out = [jax.ShapeDtypeStruct((s.part, LANES), F32)] * (s.group // 2)
    out.append(jax.ShapeDtypeStruct((s.group // 2 * s.part, LANES), BF16))
    if first:
        out.append(jax.ShapeDtypeStruct((blocks * 2 * s.part, LANES), F32))
    else:
        out += [
            jax.ShapeDtypeStruct((2 * s.part, LANES), BF16 if i % 2 else F32)
            for i in range(blocks)
        ]
    operands = list(qg) + list(kv) + ([] if first else [old])
    pairs = s.heads * s.span * blocks * s.rows
    result = pl.pallas_call(
        functools.partial(attend_kernel, s, blocks, first),
        out_shape=out,
        in_specs=[VMEM] * len(operands),
        out_specs=[VMEM] * len(out),
        scratch_shapes=[
            pltpu.VMEM((s.tiles, s.span, LANES), BF16),
            pltpu.VMEM((s.tiles, s.span, LANES), BF16),
            pltpu.VMEM((s.tiles, s.span, LANES), F32),
            pltpu.VMEM((s.group, 8, s.span_tiles * LANES), F32),
            pltpu.VMEM((s.heads, s.span_tiles * LANES), F32),
        ],
        compiler_params=pltpu.CompilerParams(vmem_limit_bytes=s.grant(blocks)),
        cost_estimate=pl.CostEstimate(
            flops=(20 if first else 200) * pairs * s.dim, bytes_accessed=4 * s.part * LANES * 8, transcendentals=pairs
        ),
    )(*operands)
    count = s.group // 2
    return result[:count], result[count], result[count + 1 :]


def core_kernel(s, keep_own, *refs):
    count = s.group // 2
    recv = refs[count]
    for i in range(count):
        total = refs[i][...] + recv[i * s.part : (i + 1) * s.part, :].astype(F32)
        refs[count + 1 + i][...] = total.astype(refs[count + 1 + i].dtype)


def core_add(s, keep, recv, keep_own):
    count = len(keep)
    out = [
        jax.ShapeDtypeStruct((s.part, LANES), F32 if keep_own and i == 0 else BF16)
        for i in range(count)
    ]
    return pl.pallas_call(
        functools.partial(core_kernel, s, keep_own),
        out_shape=out,
        in_specs=[VMEM] * (count + 1),
        out_specs=[VMEM] * count,
        compiler_params=pltpu.CompilerParams(vmem_limit_bytes=2**20),
    )(*keep, recv)


def sum_kernel(*refs):
    total = refs[0][...].astype(F32)
    for ref in refs[1:-1]:
        total = total + ref[...].astype(F32)
    refs[-1][...] = total.astype(refs[-1].dtype)


def sum_low(arrays):
    if len(arrays) == 1:
        return arrays[0] if arrays[0].dtype == BF16 else arrays[0].astype(BF16)
    return pl.pallas_call(
        sum_kernel,
        out_shape=jax.ShapeDtypeStruct(arrays[0].shape, BF16),
        in_specs=[VMEM] * len(arrays),
        out_specs=VMEM,
        compiler_params=pltpu.CompilerParams(vmem_limit_bytes=2**20),
    )(*arrays)


def sum_all(s, arrays):
    return pl.pallas_call(
        sum_kernel,
        out_shape=jax.ShapeDtypeStruct(arrays[0].shape, F32),
        in_specs=[VMEM] * len(arrays),
        out_specs=VMEM,
        compiler_params=pltpu.CompilerParams(vmem_limit_bytes=2**20),
        cost_estimate=pl.CostEstimate(flops=4000000000, bytes_accessed=0, transcendentals=0),
    )(*arrays)


def final_kernel(s, n_dq, n_kv, *refs):
    dq, kv, outs = refs[:n_dq], refs[n_dq : n_dq + n_kv], refs[n_dq + n_kv :]
    r = s.rows
    for out, sources, base in ((outs[0], dq, 0), (outs[1], kv, 0), (outs[2], kv, s.part)):
        for t in range(s.tiles):
            rows = slice(base + t * r, base + (t + 1) * r)
            total = sources[0][rows, :].astype(F32)
            for ref in sources[1:]:
                total = total + ref[rows, :].astype(F32)
            out[:, t * LANES : (t + 1) * LANES] = total.astype(BF16)


def finish(s, dq, kv):
    return pl.pallas_call(
        functools.partial(final_kernel, s, len(dq), len(kv)),
        out_shape=[jax.ShapeDtypeStruct((s.rows, s.width), BF16)] * 3,
        in_specs=[VMEM] * (len(dq) + len(kv)),
        out_specs=[VMEM] * 3,
        compiler_params=pltpu.CompilerParams(vmem_limit_bytes=2**20),
    )(*dq, *kv)


def hold(x, flops):
    return pl.pallas_call(
        lambda ref, out: None,
        out_shape=jax.ShapeDtypeStruct(x.shape, x.dtype),
        in_specs=[VMEM],
        out_specs=VMEM,
        input_output_aliases={0: 0},
        compiler_params=pltpu.CompilerParams(vmem_limit_bytes=2**20),
        cost_estimate=pl.CostEstimate(flops=flops, bytes_accessed=0, transcendentals=0),
    )(x)


def local(queries, keys, values, attended, grad_out, logsumexp):
    group, ctx = lax.axis_size("head"), lax.axis_size("ctx")
    s = Sizes(queries.shape[0], queries.shape[1], logsumexp.shape[1], group, ctx)

    def move(x, ctx_off, head_off):
        if ctx_off == 0:
            return lax.ppermute(x, "head", [(i, i ^ head_off) for i in range(group)])
        if head_off == 0:
            return lax.ppermute(x, "ctx", [(i, i ^ ctx_off) for i in range(ctx)])
        pairs = [
            (i * group + j, (i ^ ctx_off) * group + (j ^ head_off))
            for i in range(ctx)
            for j in range(group)
        ]
        return lax.ppermute(x, ("ctx", "head"), pairs)

    tie = lax.optimization_barrier
    qg_own, kv_own = pack(s, queries, keys, values, attended, grad_out, logsumexp)
    bits = [1 << i for i in reversed(range(s.high.bit_length() - 1))]
    side = group // 2
    far, kv, near = {}, {0: kv_own}, {0: qg_own}
    far[0] = move(qg_own, s.high, 0)
    kv[bits[0]] = move(kv_own, bits[0], 0)
    kv.update({bit: move(kv_own, bit, 0) for bit in bits[1:]})
    near[side] = move(qg_own, 0, side)
    kv[bits[0]] = hold(kv[bits[0]], 10000000000)
    kv[bits[-1]] = hold(kv[bits[-1]], 10000000000)
    for bit in bits:
        for off in sorted(off for off in kv if off % (2 * bit) == 0 and off):
            kv[off + bit] = move(kv[off], bit, 0)
    far[side] = move(far[0], 0, side)
    bit = side
    while bit:
        for blocks in (far, near):
            for off in sorted(off for off in blocks if off % (2 * bit) == 0):
                if off + bit not in blocks and not (blocks is far and bit == 1 and off == side):
                    blocks[off + bit] = move(blocks[off], 0, bit)
        bit //= 2
    kv = [kv[off] for off in range(s.high)]
    keep0, send0, sums0 = attend(s, [near[i] for i in range(group)], kv, None)
    keep0, send0, sums0, far = tie((keep0, send0, sums0, far))
    far[side + 1] = move(far[side], 0, 1)
    keep1, send1, sums1 = attend(s, [far[i] for i in range(group)], kv, sums0[0])
    sums1 = list(sums1)
    dq = core_add(s, keep1, move(send1, 0, 1), False)
    total_q = [move(dq[i], s.high, 2 * i) for i in range(side)]
    dq = core_add(s, keep0, move(send0, 0, 1), True)
    late_q = [move(dq[i], 0, 2 * i) for i in range(1, side)]
    late_q = total_q[1:] + late_q
    total_q = total_q[:1]
    total_q = [dq[0]] + total_q
    parts = {off: [sums1[off]] for off in range(s.high)}
    for bit in reversed(bits):
        others = [off for off in range(s.high) if off & (2 * bit - 1) == bit and off != bit]
        for off in others:
            parts[off - bit].append(move(sum_low(parts[off]), bit, 0))
        parts[0].append(move(sum_low(parts[bit]), bit, 0))
    total_q = sum_all(s, total_q)
    return tuple(finish(s, [total_q] + late_q, parts[0]))


def solution(mesh):
    rows = P(("ctx", "head"), None)
    return jax.shard_map(
        local,
        mesh=mesh,
        in_specs=(rows, rows, rows, rows, rows, P("ctx", "head")),
        out_specs=(rows, rows, rows),
        check_vma=False,
    )
```

```python
import functools
import jax
import jax.numpy as jnp
from jax import lax
from jax.experimental import pallas as pl
from jax.experimental.pallas import tpu as pltpu
from jax.sharding import PartitionSpec as P

F32 = jnp.float32
BF16 = jnp.bfloat16
LANES = 128
NT = (((1,), (1,)), ((), ()))
TN = (((0,), (0,)), ((), ()))
NN = (((1,), (0,)), ((), ()))
VMEM = pl.BlockSpec(memory_space=pltpu.VMEM)


def dot(a, b, dims):
    return lax.dot_general(a, b, dims, preferred_element_type=F32)


def round_up(n, m):
    return -(-n // m) * m


class Sizes:
    def __init__(self, rows, width, heads_group, group, ctx):
        self.rows, self.width = rows, width
        self.group, self.ctx = group, ctx
        self.heads_group = heads_group
        self.heads = heads_group * group
        self.dim = width // self.heads
        self.tiles = width // LANES
        self.span = rows * group
        self.span_tiles = -(-self.span // LANES)
        self.part = self.tiles * rows
        self.lse_rows = 2 * heads_group * self.span_tiles
        self.extra = round_up(self.lse_rows + self.heads, 16)
        self.high = ctx // 2

    def grant(self, blocks):
        scratch = 8 * self.tiles * self.span * LANES
        pairs = blocks * self.rows * round_up(self.span, LANES)
        return 2 * scratch + 48 * pairs + 2**20


def split2(x):
    hi = x.astype(BF16).astype(F32)
    return hi, x - hi


def pack_kernel(s, q_in, k_in, v_in, o_in, g_in, lse_in, qg_ref, kv_ref, *scratch):
    q_ref, k_ref, v_ref, o_ref, g_ref, lse_ref, small, side, sems = scratch
    copies = [
        pltpu.make_async_copy(source, target, sems.at[i])
        for i, (source, target) in enumerate(
            (
                (g_in, g_ref),
                (o_in, o_ref),
                (lse_in, lse_ref),
                (q_in, q_ref),
                (k_in, k_ref),
                (v_in, v_ref),
            )
        )
    ]
    for copy in copies:
        copy.start()
    r = s.rows
    copies[0].wait()
    copies[1].wait()
    prod = g_ref[...].astype(F32) * o_ref[...].astype(F32)
    hi = prod.astype(BF16)
    lo = (prod - hi.astype(F32)).astype(BF16)
    shape = (round_up(s.heads, 16), s.width)
    pick = lax.broadcasted_iota(jnp.int32, shape, 1) // s.dim
    pick = (pick == lax.broadcasted_iota(jnp.int32, shape, 0)).astype(F32).astype(BF16)
    delta = dot(pick, hi, NT) + dot(pick, lo, NT)
    d_hi, d_low = split2(delta)
    small[...] = jnp.zeros(small.shape, F32)
    side[...] = jnp.zeros(side.shape, F32)
    side[:, :r] = d_low
    d_low = pltpu.roll(side[...], LANES // 2, 1)
    side[:, :r] = d_hi
    deltas = side[...] + d_low
    copies[2].wait()
    h = s.heads_group
    at = 0
    for t in range(s.span_tiles):
        lanes = min(LANES, s.span - t * LANES)
        for piece in split2(lse_ref[:, t * LANES : t * LANES + lanes]):
            small[at : at + h, :lanes] = piece
            at += h
    small[at : at + s.heads, :] = deltas[: s.heads]
    qg_ref[2 * s.part :, :] = small[...].astype(BF16)
    for copy in copies[3:]:
        copy.wait()
    for t in range(s.tiles):
        lanes = slice(t * LANES, (t + 1) * LANES)
        rows = slice(t * r, (t + 1) * r)
        more = slice(s.part + t * r, s.part + (t + 1) * r)
        qg_ref[rows, :] = (q_ref[:, lanes].astype(F32) * s.dim**-0.5).astype(BF16)
        qg_ref[more, :] = g_ref[:, lanes]
        kv_ref[rows, :] = k_ref[:, lanes]
        kv_ref[more, :] = v_ref[:, lanes]


def in_hbm(x):
    return pltpu.with_memory_space_constraint(x, pltpu.HBM)


def pack(s, q, k, v, o, g, lse):
    return pl.pallas_call(
        functools.partial(pack_kernel, s),
        out_shape=(
            jax.ShapeDtypeStruct((2 * s.part + s.extra, LANES), BF16),
            jax.ShapeDtypeStruct((2 * s.part, LANES), BF16),
        ),
        in_specs=[pl.BlockSpec(memory_space=pl.ANY)] * 6,
        out_specs=[VMEM] * 2,
        scratch_shapes=[pltpu.VMEM((s.rows, s.width), BF16)] * 5
        + [
            pltpu.VMEM((s.heads_group, s.span), F32),
            pltpu.VMEM((s.extra, LANES), F32),
            pltpu.VMEM((round_up(s.heads, 16), LANES), F32),
            pltpu.SemaphoreType.DMA((6,)),
        ],
        compiler_params=pltpu.CompilerParams(vmem_limit_bytes=2 * 2**20),
    )(*[in_hbm(x) for x in (q, k, v, o, g, jnp.transpose(lse))])


def attend_kernel(s, blocks, first, *refs):
    r, n = s.rows, s.group
    refs = list(refs)
    take = lambda count: [refs.pop(0) for _ in range(count)]
    qg, kv = take(n), take(blocks)
    (old,) = take(1) if not first else (None,)
    keep, (send,) = take(n // 2), take(1)
    sums = take(1 if first else blocks)
    qs, gs, dqs, norms, deltas = refs
    me = lax.axis_index("head")
    scale = s.dim**-0.5
    wide = s.span_tiles * LANES
    h = s.heads_group
    total = jnp.zeros((s.heads, wide), F32)
    used = lax.broadcasted_iota(jnp.int32, (s.heads, LANES), 1) < r
    for off in range(n):
        who = lax.bitwise_xor(me, off)
        at = pl.multiple_of(who * r, 16)
        for t in range(s.tiles):
            qs[t, pl.ds(at, r), :] = qg[off][t * r : (t + 1) * r, :]
            gs[t, pl.ds(at, r), :] = qg[off][s.part + t * r : s.part + (t + 1) * r, :]
        small = qg[off][2 * s.part :, :].astype(F32)
        pieces = []
        for t in range(s.span_tiles):
            b = 2 * h * t
            pieces.append(small[b : b + h] + small[b + h : b + 2 * h])
        norms[who, :h, :] = jnp.concatenate(pieces, axis=1)
        b = s.lse_rows
        delta = small[b : b + s.heads]
        delta = jnp.where(used, delta + pltpu.roll(delta, LANES // 2, 1), 0.0)
        if wide > LANES:
            delta = jnp.concatenate([delta, jnp.zeros((s.heads, wide - LANES), F32)], axis=1)
        total = total + pltpu.roll(delta, who * r, 1)
    deltas[...] = total
    size = blocks * r
    lane = lax.broadcasted_iota(jnp.int32, (2 * size, LANES), 1) < s.dim
    first_head = lax.broadcasted_iota(jnp.int32, (2 * size, LANES), 0) < size
    own_lanes = lane == first_head
    half = lane[:size]
    zero = jnp.zeros((), BF16)

    def pair(block):
        return jnp.where(own_lanes, jnp.concatenate([block, block], axis=0), zero)

    def front(t):
        rows = slice(t * r, (t + 1) * r)
        more = slice(s.part + t * r, s.part + (t + 1) * r)
        k = pair(jnp.concatenate([ref[rows, :] for ref in kv], axis=0))
        v = pair(jnp.concatenate([ref[more, :] for ref in kv], axis=0))
        return k, dot(k, qs[t], NT), dot(v, gs[t], NT)

    def middle(t, scores, dweights):
        low, dscores = [], []
        for e in range(2):
            head = 2 * t + e
            mine = slice(e * size, (e + 1) * size)
            j = head % h
            weights = jnp.exp(scores[mine] - norms[head // h, j : j + 1, : s.span])
            low.append(weights.astype(BF16))
            gap = dweights[mine] - deltas[head : head + 1, : s.span]
            dscores.append((weights * gap).astype(BF16))
        return jnp.concatenate(low, axis=0), jnp.concatenate(dscores, axis=0)

    def back(t, k, low, dscores):
        rows = slice(t * r, (t + 1) * r)
        more = slice(s.part + t * r, s.part + (t + 1) * r)
        dv = dot(low, gs[t], NN)
        dk = dot(dscores, qs[t], NN)
        dv, dk = [dv[:size], dv[size:]], [dk[:size], dk[size:]]
        dqs[t] = dot(k, dscores, TN).T * scale
        for where, parts in ((rows, dk), (more, dv)):
            both = jnp.where(half, parts[0], parts[1])
            for i in range(blocks):
                piece = both[i * r : (i + 1) * r]
                if first:
                    sums[0][2 * s.part * i + where.start : 2 * s.part * i + where.stop, :] = piece
                else:
                    piece = piece + old[2 * s.part * i + where.start : 2 * s.part * i + where.stop, :]
                    sums[i][where, :] = piece.astype(sums[i].dtype)

    ahead = [front(t) for t in range(min(2, s.tiles))]
    for t in range(s.tiles):
        k, scores, dweights = ahead.pop(0)
        if t + 2 < s.tiles:
            ahead.append(front(t + 2))
        back(t, k, *middle(t, scores, dweights))
    for off in range(n):
        at = pl.multiple_of(lax.bitwise_xor(me, off) * r, 16)
        for t in range(s.tiles):
            piece = dqs[t, pl.ds(at, r), :]
            i = off // 2
            if off % 2 == 0:
                keep[i][t * r : (t + 1) * r, :] = piece
            else:
                send[i * s.part + t * r : i * s.part + (t + 1) * r, :] = piece.astype(BF16)


def attend(s, qg, kv, old):
    blocks = len(kv)
    first = old is None
    out = [jax.ShapeDtypeStruct((s.part, LANES), F32)] * (s.group // 2)
    out.append(jax.ShapeDtypeStruct((s.group // 2 * s.part, LANES), BF16))
    if first:
        out.append(jax.ShapeDtypeStruct((blocks * 2 * s.part, LANES), F32))
    else:
        out += [
            jax.ShapeDtypeStruct((2 * s.part, LANES), BF16 if i % 2 else F32)
            for i in range(blocks)
        ]
    operands = list(qg) + list(kv) + ([] if first else [old])
    pairs = s.heads * s.span * blocks * s.rows
    result = pl.pallas_call(
        functools.partial(attend_kernel, s, blocks, first),
        out_shape=out,
        in_specs=[VMEM] * len(operands),
        out_specs=[VMEM] * len(out),
        scratch_shapes=[
            pltpu.VMEM((s.tiles, s.span, LANES), BF16),
            pltpu.VMEM((s.tiles, s.span, LANES), BF16),
            pltpu.VMEM((s.tiles, s.span, LANES), F32),
            pltpu.VMEM((s.group, 8, s.span_tiles * LANES), F32),
            pltpu.VMEM((s.heads, s.span_tiles * LANES), F32),
        ],
        compiler_params=pltpu.CompilerParams(vmem_limit_bytes=s.grant(blocks)),
        cost_estimate=pl.CostEstimate(
            flops=(20 if first else 200) * pairs * s.dim, bytes_accessed=4 * s.part * LANES * 8, transcendentals=pairs
        ),
    )(*operands)
    count = s.group // 2
    return result[:count], result[count], result[count + 1 :]


def core_kernel(s, keep_own, *refs):
    count = s.group // 2
    recv = refs[count]
    for i in range(count):
        total = refs[i][...] + recv[i * s.part : (i + 1) * s.part, :].astype(F32)
        refs[count + 1 + i][...] = total.astype(refs[count + 1 + i].dtype)


def core_add(s, keep, recv, keep_own):
    count = len(keep)
    out = [
        jax.ShapeDtypeStruct((s.part, LANES), F32 if keep_own and i == 0 else BF16)
        for i in range(count)
    ]
    return pl.pallas_call(
        functools.partial(core_kernel, s, keep_own),
        out_shape=out,
        in_specs=[VMEM] * (count + 1),
        out_specs=[VMEM] * count,
        compiler_params=pltpu.CompilerParams(vmem_limit_bytes=2**20),
    )(*keep, recv)


def sum_kernel(*refs):
    total = refs[0][...].astype(F32)
    for ref in refs[1:-1]:
        total = total + ref[...].astype(F32)
    refs[-1][...] = total.astype(refs[-1].dtype)


def sum_low(arrays):
    if len(arrays) == 1:
        return arrays[0] if arrays[0].dtype == BF16 else arrays[0].astype(BF16)
    return pl.pallas_call(
        sum_kernel,
        out_shape=jax.ShapeDtypeStruct(arrays[0].shape, BF16),
        in_specs=[VMEM] * len(arrays),
        out_specs=VMEM,
        compiler_params=pltpu.CompilerParams(vmem_limit_bytes=2**20),
    )(*arrays)


def sum_all(s, arrays):
    return pl.pallas_call(
        sum_kernel,
        out_shape=jax.ShapeDtypeStruct(arrays[0].shape, F32),
        in_specs=[VMEM] * len(arrays),
        out_specs=VMEM,
        compiler_params=pltpu.CompilerParams(vmem_limit_bytes=2**20),
        cost_estimate=pl.CostEstimate(flops=4000000000, bytes_accessed=0, transcendentals=0),
    )(*arrays)


def final_kernel(s, n_dq, n_kv, *refs):
    dq, kv, outs = refs[:n_dq], refs[n_dq : n_dq + n_kv], refs[n_dq + n_kv :]
    r = s.rows
    for out, sources, base in ((outs[0], dq, 0), (outs[1], kv, 0), (outs[2], kv, s.part)):
        for t in range(s.tiles):
            rows = slice(base + t * r, base + (t + 1) * r)
            total = sources[0][rows, :].astype(F32)
            for ref in sources[1:]:
                total = total + ref[rows, :].astype(F32)
            out[:, t * LANES : (t + 1) * LANES] = total.astype(BF16)


def finish(s, dq, kv):
    return pl.pallas_call(
        functools.partial(final_kernel, s, len(dq), len(kv)),
        out_shape=[jax.ShapeDtypeStruct((s.rows, s.width), BF16)] * 3,
        in_specs=[VMEM] * (len(dq) + len(kv)),
        out_specs=[VMEM] * 3,
        compiler_params=pltpu.CompilerParams(vmem_limit_bytes=2**20),
    )(*dq, *kv)


def hold(x, flops):
    return pl.pallas_call(
        lambda ref, out: None,
        out_shape=jax.ShapeDtypeStruct(x.shape, x.dtype),
        in_specs=[VMEM],
        out_specs=VMEM,
        input_output_aliases={0: 0},
        compiler_params=pltpu.CompilerParams(vmem_limit_bytes=2**20),
        cost_estimate=pl.CostEstimate(flops=flops, bytes_accessed=0, transcendentals=0),
    )(x)


def local(queries, keys, values, attended, grad_out, logsumexp):
    group, ctx = lax.axis_size("head"), lax.axis_size("ctx")
    s = Sizes(queries.shape[0], queries.shape[1], logsumexp.shape[1], group, ctx)

    def move(x, ctx_off, head_off):
        if ctx_off == 0:
            return lax.ppermute(x, "head", [(i, i ^ head_off) for i in range(group)])
        if head_off == 0:
            return lax.ppermute(x, "ctx", [(i, i ^ ctx_off) for i in range(ctx)])
        pairs = [
            (i * group + j, (i ^ ctx_off) * group + (j ^ head_off))
            for i in range(ctx)
            for j in range(group)
        ]
        return lax.ppermute(x, ("ctx", "head"), pairs)

    tie = lax.optimization_barrier
    qg_own, kv_own = pack(s, queries, keys, values, attended, grad_out, logsumexp)
    bits = [1 << i for i in reversed(range(s.high.bit_length() - 1))]
    side = group // 2
    far, kv, near = {}, {0: kv_own}, {0: qg_own}
    far[0] = move(qg_own, s.high, 0)
    kv[bits[0]] = move(kv_own, bits[0], 0)
    kv.update({bit: move(kv_own, bit, 0) for bit in bits[1:]})
    near[side] = move(qg_own, 0, side)
    kv[bits[0]] = hold(kv[bits[0]], 10000000000)
    kv[bits[-1]] = hold(kv[bits[-1]], 10000000000)
    for bit in bits:
        for off in sorted(off for off in kv if off % (2 * bit) == 0 and off):
            kv[off + bit] = move(kv[off], bit, 0)
    far[side] = move(far[0], 0, side)
    bit = side
    while bit:
        for blocks in (far, near):
            for off in sorted(off for off in blocks if off % (2 * bit) == 0):
                if off + bit not in blocks and not (blocks is far and bit == 1 and off == side):
                    blocks[off + bit] = move(blocks[off], 0, bit)
        bit //= 2
    kv = [kv[off] for off in range(s.high)]
    keep0, send0, sums0 = attend(s, [near[i] for i in range(group)], kv, None)
    keep0, send0, sums0, far = tie((keep0, send0, sums0, far))
    far[side + 1] = move(far[side], 0, 1)
    keep1, send1, sums1 = attend(s, [far[i] for i in range(group)], kv, sums0[0])
    sums1 = list(sums1)
    dq = core_add(s, keep1, move(send1, 0, 1), False)
    total_q = [move(dq[i], s.high, 2 * i) for i in range(side)]
    dq = core_add(s, keep0, move(send0, 0, 1), True)
    late_q = [move(dq[i], 0, 2 * i) for i in range(1, side)]
    late_q = total_q[1:] + late_q
    total_q = total_q[:1]
    total_q = [dq[0]] + total_q
    sums1 = list(sums1)
    sums1[-1], near_dq = tie((sums1[-1], late_q[-1]))
    late_q[-1] = near_dq
    parts = {off: [sums1[off]] for off in range(s.high)}
    for bit in reversed(bits):
        others = [off for off in range(s.high) if off & (2 * bit - 1) == bit and off != bit]
        for off in others:
            parts[off - bit].append(move(sum_low(parts[off]), bit, 0))
        parts[0].append(move(sum_low(parts[bit]), bit, 0))
    total_q = sum_all(s, total_q)
    return tuple(finish(s, [total_q] + late_q, parts[0]))


def solution(mesh):
    rows = P(("ctx", "head"), None)
    return jax.shard_map(
        local,
        mesh=mesh,
        in_specs=(rows, rows, rows, rows, rows, P("ctx", "head")),
        out_specs=(rows, rows, rows),
        check_vma=False,
    )
```
